256 devices in a mesh: seq: 64 (over z, y, x_hi), head: 4 (over x_lo, core).
Axes of the slice: x: 4 (x_hi: 2, x_lo: 2; x = x_hi * 2 + x_lo), y: 4, z: 8, core: 2. Of those that a mesh axis runs over, the one named last changes fastest.
Arguments:
- queries: bfloat16 [32768, 2048], P(('seq', 'head')), may hold values from -6 to 6
- key_rows: bfloat16 [32768, 2048], P(('seq', 'head')), may hold values from -6 to 6
- value_rows: bfloat16 [32768, 2048], P(('seq', 'head')), may hold values from -6 to 6
- cotangent: bfloat16 [32768, 2048], P(('seq', 'head')), may hold values from -192 to 192
- cluster_of: int32 [32768], P('seq'), may hold values from 0 to 127, as said below
- order_tokens: int32 [32768], P('seq'), may hold values from 0 to 32767, as said below
Outputs:
- attended: bfloat16 [32768, 2048], P(('seq', 'head'))
- grad_queries: bfloat16 [32768, 2048], P(('seq', 'head'))
- grad_keys: bfloat16 [32768, 2048], P(('seq', 'head'))
- grad_values: bfloat16 [32768, 2048], P(('seq', 'head'))
The draws below stay inside these ranges and needn't reach their ends.
Inputs may be any that keep to these rules, and one draw needn't show every extreme that they name: `cluster_of`: each of the 128 clusters holds exactly 256 tokens. Cluster c belongs to owner c // 2 along seq; the 512 tokens of one index of seq lie in the clusters of one owner at most 10 times, and exactly 10 times for some index and owner. Each token appears once; the tokens of cluster 0 come first, then those of cluster 1 and so on: cluster_of[order_tokens[p]] = p // 256.
All inputs are finite; a program needn't handle non-finite values.
Results may differ from the reference program's by a relative error of at most 0.0068.
The reference program's roundings to bfloat16 on the way count: a program that leaves them out, or rounds other values in their place, can miss the bound.
Values may be sent and summed in bfloat16 or wider, within the bound.
A program may use at most 64 MiB of HBM per device.

```python
import jax
import jax.numpy as jnp
from jax import lax

HEADS = 16
DH = 128
CLUSTER = 256
TOK_DEV = 512
TOKENS = 32768
NCLUST = 128
N_SEQ = 64


def shuffled(sub_key):
    return jax.random.permutation(sub_key, TOK_DEV)


def routing_tables(key):
    pair_key, amount_key, row_key, col_key, order_key, spin_key = jax.random.split(key, 6)
    mean_count = TOK_DEV // N_SEQ
    spread = mean_count // 4
    halves = N_SEQ // 2
    pairing = jax.random.permutation(pair_key, N_SEQ)
    moved_count = jax.random.randint(amount_key, (halves,), 0, spread + 1).at[0].set(spread)
    weights = jnp.full((N_SEQ,), mean_count, jnp.int32)
    weights = weights.at[pairing[:halves]].add(moved_count).at[pairing[halves:]].add(-moved_count)
    row_perm = jax.random.permutation(row_key, N_SEQ)
    col_perm = jax.random.permutation(col_key, N_SEQ)
    counts = weights[(col_perm[None, :] - row_perm[:, None]) % N_SEQ]
    row_end = jnp.cumsum(counts, axis=1)
    row_start = row_end - counts
    col_start = jnp.cumsum(counts, axis=0) - counts
    rank_rows = jnp.arange(TOK_DEV, dtype=jnp.int32)
    target = jnp.sum((row_end[:, None, :] <= rank_rows[None, :, None]).astype(jnp.int32), axis=-1)
    within = rank_rows[None, :] - jnp.take_along_axis(row_start, target, axis=1)
    slot_rows = jnp.take_along_axis(col_start, target, axis=1) + within
    orders = jax.vmap(shuffled)(jax.random.split(order_key, N_SEQ))
    spin_tables = jax.vmap(shuffled)(jax.random.split(spin_key, N_SEQ))
    spun_slot = spin_tables[target, slot_rows]
    position = target * TOK_DEV + spun_slot
    tokens = jnp.arange(N_SEQ, dtype=jnp.int32)[:, None] * TOK_DEV + orders
    order_tokens = jnp.zeros((TOKENS,), jnp.int32).at[position.reshape(-1)].set(tokens.reshape(-1))
    cluster_of = jnp.zeros((TOKENS,), jnp.int32).at[tokens.reshape(-1)].set((position // CLUSTER).reshape(-1))
    return (cluster_of, order_tokens)


def centroids(key, salt):
    return jax.random.normal(jax.random.fold_in(key, salt), (NCLUST, HEADS * DH))


def draw_cluster_of(key, part):
    return routing_tables(key)[0]


def draw_order_tokens(key, part):
    return routing_tables(key)[1]


def draw_queries(key, part):
    cluster_ids = routing_tables(key)[0]
    shared = centroids(key, 101)
    key = jax.random.fold_in(key, 1)
    link_key, noise_key = jax.random.split(key, 2)
    linked = jax.random.randint(link_key, (TOKENS,), 0, NCLUST)
    extent = (TOKENS, HEADS * DH)
    jitter = jax.random.normal(noise_key, extent)
    field = 0.25 * shared[cluster_ids] + 0.85 * shared[linked] + 0.45 * jitter
    return jnp.clip(field, -6.0, 6.0).astype(jnp.bfloat16)


def draw_key_rows(key, part):
    cluster_ids = routing_tables(key)[0]
    shared = centroids(key, 101)
    key = jax.random.fold_in(key, 2)
    noise_key = jax.random.fold_in(key, 0)
    extent = (TOKENS, HEADS * DH)
    jitter = jax.random.normal(noise_key, extent)
    field = 0.6 * shared[cluster_ids] + 0.8 * jitter
    return jnp.clip(field, -6.0, 6.0).astype(jnp.bfloat16)


def draw_value_rows(key, part):
    cluster_ids = routing_tables(key)[0]
    key = jax.random.fold_in(key, 3)
    own_centres = centroids(key, 105)
    noise_key = jax.random.fold_in(key, 7)
    extent = (TOKENS, HEADS * DH)
    jitter = jax.random.normal(noise_key, extent)
    field = 0.6 * own_centres[cluster_ids] + 0.8 * jitter
    return jnp.clip(field, -6.0, 6.0).astype(jnp.bfloat16)


def levels(rng, shape, pieces, low, top_value):
    def one(axis_at, parts):
        steps = jax.random.uniform(jax.random.fold_in(jax.random.fold_in(rng, 6), axis_at), (parts,), jnp.float32, low / len(pieces), top_value / len(pieces))
        return jnp.repeat(jnp.exp(steps), shape[axis_at] // parts).reshape((-1,) + (1,) * (len(shape) - axis_at - 1))

    loudness = one(*pieces[0])
    for cut in pieces[1:]:
        loudness = loudness * one(*cut)
    return loudness


def centred(rng, shape, scale, limit, pieces=(), kind=jnp.bfloat16):
    values = scale * jax.random.normal(rng, shape, jnp.float32)
    if pieces:
        values = values * levels(rng, shape, pieces, -0.22, 0.18)
    return jnp.clip(values, -limit, limit).astype(kind)


def setup_inputs(seed: int = 0) -> dict:
    keys = jax.random.split(jax.random.key(seed), 7)
    return {
        "queries": draw_queries(jax.random.fold_in(keys[6], 71), 0),
        "key_rows": draw_key_rows(jax.random.fold_in(keys[6], 71), 0),
        "value_rows": draw_value_rows(jax.random.fold_in(keys[6], 71), 0),
        "cotangent": centred(keys[3], (TOKENS, HEADS * DH), 32.0, 192.0, ((0, 256),)),
        "cluster_of": draw_cluster_of(jax.random.fold_in(keys[6], 71), 0),
        "order_tokens": draw_order_tokens(jax.random.fold_in(keys[6], 71), 0),
    }


def reference(queries, key_rows, value_rows, cotangent, cluster_of, order_tokens):
    width = HEADS * DH
    score_scale = DH ** -0.5
    owned_count = TOK_DEV // CLUSTER

    def cluster_means(field):
        split_heads = field.reshape(TOKENS, HEADS, DH).transpose(1, 0, 2)

        def one_head(column):
            return jax.ops.segment_sum(column.astype(jnp.float32), cluster_of, num_segments=NCLUST)

        summed = lax.map(one_head, split_heads)
        return (summed.transpose(1, 0, 2) / CLUSTER).astype(jnp.bfloat16)

    key_means = cluster_means(key_rows).astype(jnp.float32)
    value_means = cluster_means(value_rows).astype(jnp.float32)

    def sorted_blocks(field):
        return field[order_tokens].reshape(N_SEQ, TOK_DEV, HEADS, DH)

    def block_step(carry, item):
        key_acc, value_acc = carry
        block_q, block_k, block_v, block_g, block_tok = item
        query_rows = block_q.astype(jnp.float32)
        grad_rows = block_g.astype(jnp.float32)
        query_cells = query_rows.reshape(owned_count, CLUSTER, HEADS, DH)
        key_cells = block_k.astype(jnp.float32).reshape(owned_count, CLUSTER, HEADS, DH)
        value_cells = block_v.astype(jnp.float32).reshape(owned_count, CLUSTER, HEADS, DH)
        grad_cells = grad_rows.reshape(owned_count, CLUSTER, HEADS, DH)
        tok_cells = block_tok.reshape(owned_count, CLUSTER)
        visible = tok_cells[:, None, :] <= tok_cells[:, :, None]
        inner = jnp.einsum("cihd,cjhd->hcij", query_cells, key_cells) * score_scale
        outer = jnp.einsum("phd,nhd->hpn", query_rows, key_means) * score_scale
        inner_top = jnp.max(jnp.where(visible, inner, -jnp.inf), axis=-1)
        row_top = jnp.maximum(inner_top, jnp.max(outer, axis=-1).reshape(HEADS, owned_count, CLUSTER))
        inner_exp = jnp.where(visible, jnp.exp(inner - row_top[..., None]), 0.0)
        outer_exp = jnp.exp(outer - row_top.reshape(HEADS, TOK_DEV)[..., None])
        row_total = jnp.sum(inner_exp, axis=-1) + jnp.sum(outer_exp, axis=-1).reshape(HEADS, owned_count, CLUSTER)
        inner_weight = inner_exp / row_total[..., None]
        outer_weight = outer_exp / row_total.reshape(HEADS, TOK_DEV)[..., None]
        inner_round = lax.optimization_barrier(inner_weight.astype(jnp.bfloat16)).astype(jnp.float32)
        outer_round = lax.optimization_barrier(outer_weight.astype(jnp.bfloat16)).astype(jnp.float32)
        mixed = jnp.einsum("hcij,cjhd->cihd", inner_round, value_cells).reshape(TOK_DEV, HEADS, DH)
        mixed = mixed + jnp.einsum("hpn,nhd->phd", outer_round, value_means)
        inner_grad = jnp.einsum("cihd,cjhd->hcij", grad_cells, value_cells)
        outer_grad = jnp.einsum("phd,nhd->hpn", grad_rows, value_means)
        row_delta = jnp.sum(inner_weight * inner_grad, axis=-1)
        row_delta = row_delta + jnp.sum(outer_weight * outer_grad, axis=-1).reshape(HEADS, owned_count, CLUSTER)
        inner_step = inner_weight * (inner_grad - row_delta[..., None])
        inner_step = lax.optimization_barrier(inner_step.astype(jnp.bfloat16)).astype(jnp.float32)
        outer_step = outer_weight * (outer_grad - row_delta.reshape(HEADS, TOK_DEV)[..., None])
        outer_step = lax.optimization_barrier(outer_step.astype(jnp.bfloat16)).astype(jnp.float32)
        grad_query = jnp.einsum("hcij,cjhd->cihd", inner_step, key_cells).reshape(TOK_DEV, HEADS, DH)
        grad_query = score_scale * (grad_query + jnp.einsum("hpn,nhd->phd", outer_step, key_means))
        grad_key_inner = score_scale * jnp.einsum("hcij,cihd->cjhd", inner_step, query_cells)
        grad_value_inner = jnp.einsum("hcij,cihd->cjhd", inner_round, grad_cells)
        key_acc = key_acc + score_scale * jnp.einsum("hpn,phd->nhd", outer_step, query_rows)
        value_acc = value_acc + jnp.einsum("hpn,phd->nhd", outer_round, grad_rows)
        outputs = (mixed.astype(jnp.bfloat16), grad_query.astype(jnp.bfloat16),
                   grad_key_inner.reshape(TOK_DEV, HEADS, DH), grad_value_inner.reshape(TOK_DEV, HEADS, DH))
        return (key_acc, value_acc), outputs

    start = (jnp.zeros((NCLUST, HEADS, DH), jnp.float32), jnp.zeros((NCLUST, HEADS, DH), jnp.float32))
    items = (sorted_blocks(queries), sorted_blocks(key_rows), sorted_blocks(value_rows),
             sorted_blocks(cotangent), order_tokens.reshape(N_SEQ, TOK_DEV))
    (key_acc, value_acc), stacked = lax.scan(block_step, start, items)

    def unsort(field):
        return jnp.zeros((TOKENS, width), field.dtype).at[order_tokens].set(field.reshape(TOKENS, width))

    attended = unsort(stacked[0])
    grad_queries = unsort(stacked[1])
    mean_key_grads = key_acc.reshape(NCLUST, width)
    mean_value_grads = value_acc.reshape(NCLUST, width)
    grad_keys = (unsort(stacked[2]) + mean_key_grads[cluster_of] / CLUSTER).astype(jnp.bfloat16)
    grad_values = (unsort(stacked[3]) + mean_value_grads[cluster_of] / CLUSTER).astype(jnp.bfloat16)
    return (attended, grad_queries, grad_keys, grad_values)
```

```python
import functools

import jax
import jax.numpy as jnp
from jax import lax
from jax.experimental import pallas as pl
from jax.experimental.pallas import tpu as pltpu
from jax.sharding import PartitionSpec as P

DH = 128
CLUSTER = 256
MESH = pl.DeviceIdType.MESH
F32 = jnp.float32
BF16 = jnp.bfloat16

TILE = 32


def dot(a, b, dims=((1,), (0,))):
    return lax.dot_general(a, b, (dims, ((), ())), preferred_element_type=F32)


def as_column(row):
    return jnp.transpose(jnp.broadcast_to(row, (128, row.shape[1])))[:, :1]


def slot_vectors(group, rank_key, capacity):
    group_col, key_col = as_column(group), as_column(rank_key)
    same = group_col == group
    rank_col = jnp.sum(jnp.where(same & (rank_key < key_col), 1.0, 0.0), axis=1, keepdims=True)
    rank_row = jnp.sum(jnp.where(same & (key_col < rank_key), 1.0, 0.0), axis=0, keepdims=True)
    return group * capacity + rank_row, group_col * capacity + rank_col


def one_hot_rows(slot_row, count):
    slots = lax.broadcasted_iota(jnp.int32, (count, slot_row.shape[1]), 0).astype(F32)
    return jnp.where(slots == slot_row, 1.0, 0.0).astype(BF16)


def one_hot_columns(slot_col, count):
    slots = lax.broadcasted_iota(jnp.int32, (slot_col.shape[0], count), 1).astype(F32)
    return jnp.where(slots == slot_col, 1.0, 0.0).astype(BF16)


def kernel(
    seq_count, head_count, heads, capacity,
    q_ref, k_ref, v_ref, g_ref, cluster_ref, order_ref,
    out_a, out_q, out_k, out_v,
    home, mid, send_buf, recv_buf, owned, mean_msg, mean_buf, means,
    results, inner, mean_acc, grad_msg, grad_buf, grad_sum, back_send, back_recv, home_out,
    spread, gather, unsort, resort, tile_perm, tile_back, hidden,
    home_send, home_recv, there_send, there_recv, mean_send, mean_recv, grad_send, grad_recv,
    back_send_sem, back_recv_sem, out_send, out_recv,
):
    me = lax.axis_index("seq")
    my_head = lax.axis_index("head")
    combos = 2 * heads
    width = heads * DH
    rows = q_ref.shape[0]
    group_rows = rows * head_count
    owned_count = group_rows // CLUSTER
    slots = seq_count * capacity
    block = capacity * combos
    mean_rows = owned_count * combos
    mean_count = seq_count * owned_count
    scale = DH ** (-0.5)
    pairs = combos // 2

    def peer(step):
        return lax.rem(me + step, seq_count)

    def head_peer(step):
        return lax.rem(my_head + step, head_count)

    barrier = pltpu.get_barrier_semaphore()

    @pl.loop(1, head_count)
    def _(step):
        pl.semaphore_signal(
            barrier, inc=1, device_id={"head": head_peer(step)}, device_id_type=MESH
        )

    @pl.loop(1, seq_count)
    def _(step):
        pl.semaphore_signal(barrier, inc=1, device_id={"seq": peer(step)}, device_id_type=MESH)

    pl.semaphore_wait(barrier, head_count - 1 + seq_count - 1)

    def wait_bytes(ref, semaphore):
        pltpu.make_async_copy(ref, ref, semaphore).wait()

    my_rows = pl.ds(pl.multiple_of(my_head * rows, rows), rows)
    my_lanes = pl.ds(pl.multiple_of(my_head * width, width), width)
    arrays = (k_ref, v_ref, q_ref, g_ref)
    for index, ref in enumerate(arrays):
        chunk = index // 2

        @pl.loop(1, head_count)
        def _(step, index=index, ref=ref, chunk=chunk):
            other = head_peer(step)
            pltpu.make_async_remote_copy(
                src_ref=ref.at[:, pl.ds(pl.multiple_of(other * width, width), width)],
                dst_ref=home.at[index, my_rows],
                send_sem=home_send.at[chunk],
                recv_sem=home_recv.at[chunk],
                device_id={"head": other},
                device_id_type=MESH,
            ).start()

        home[index, my_rows, :] = ref[:, my_lanes]

    target = (cluster_ref[...] // owned_count).astype(F32)
    position = lax.broadcasted_iota(jnp.int32, (1, group_rows), 1).astype(F32)
    row, column = slot_vectors(target, position, capacity)
    spread[...] = one_hot_rows(row, slots)
    gather[...] = one_hot_columns(column, slots)
    tokens_int = order_ref[...]
    tokens = tokens_int.astype(F32)
    row, column = slot_vectors((tokens_int // group_rows).astype(F32), tokens, capacity)
    unsort[...] = one_hot_rows(row, slots)
    resort[...] = one_hot_columns(column, slots)
    side = TILE * combos
    first = lax.broadcasted_iota(jnp.int32, (side, side), 0)
    second = lax.broadcasted_iota(jnp.int32, (side, side), 1)
    tile_perm[...] = jnp.where(
        second == (first % combos) * TILE + first // combos, 1.0, 0.0
    ).astype(BF16)
    tile_back[...] = jnp.where(
        first == (second % combos) * TILE + second // combos, 1.0, 0.0
    ).astype(BF16)
    for c in range(owned_count):
        part = tokens[:, c * CLUSTER : (c + 1) * CLUSTER]
        hidden[c] = jnp.where(as_column(part) <= part, 0.0, -jnp.inf)
    if mean_buf.shape[0] > seq_count * mean_rows:
        mean_buf[...] = jnp.zeros_like(mean_buf)

    def pack(one_hot, source, target_ref, chunk):
        for i in range(pairs):
            mid[i] = dot(one_hot[...], source(i)).astype(BF16)

        @pl.loop(0, slots // (2 * TILE))
        def _(g):
            at = pl.multiple_of(g * 2 * TILE, 2 * TILE)
            halves = []
            for half in range(2):
                pieces = []
                for i in range(pairs):
                    piece = mid[i, pl.ds(at + half * TILE, TILE), :]
                    pieces += [piece[:, :DH], piece[:, DH:]]
                halves.append(jnp.concatenate(pieces, axis=0))
            moved = dot(tile_perm[...], jnp.concatenate(halves, axis=1)).astype(BF16)
            to = pl.multiple_of(g * 2 * side, 2 * side)
            target_ref[chunk, pl.ds(to, side), :] = moved[:, :DH]
            target_ref[chunk, pl.ds(to + side, side), :] = moved[:, DH:]

    def unpack(source_ref, chunk, one_hot, sink):
        @pl.loop(0, slots // (2 * TILE))
        def _(g):
            at = pl.multiple_of(g * 2 * TILE, 2 * TILE)
            start = pl.multiple_of(g * 2 * side, 2 * side)
            both = jnp.concatenate(
                [source_ref[chunk, pl.ds(start, side), :], source_ref[chunk, pl.ds(start + side, side), :]],
                axis=1,
            )
            moved = dot(tile_back[...], both).astype(BF16)
            for half in range(2):
                lanes = slice(half * DH, (half + 1) * DH)
                for i in range(pairs):
                    low = moved[2 * i * TILE : (2 * i + 1) * TILE, lanes]
                    high = moved[(2 * i + 1) * TILE : (2 * i + 2) * TILE, lanes]
                    mid[i, pl.ds(at + half * TILE, TILE), :] = jnp.concatenate([low, high], axis=1)

        for i in range(pairs):
            sink(i, dot(one_hot[...], mid[i]).astype(BF16))

    def exchange(source_ref, dest_ref, size, send_sem, recv_sem):
        mine = pl.ds(pl.multiple_of(me * size, size), size)

        @pl.loop(1, seq_count)
        def _(step):
            other = peer(step)
            pltpu.make_async_remote_copy(
                src_ref=source_ref.at[pl.ds(pl.multiple_of(other * size, size), size)],
                dst_ref=dest_ref.at[mine],
                send_sem=send_sem,
                recv_sem=recv_sem,
                device_id={"seq": other},
                device_id_type=MESH,
            ).start()

        dest_ref[mine, :] = source_ref[mine, :]

    def wait_exchange(ref, size, semaphore):
        wait_bytes(ref.at[pl.ds(0, (seq_count - 1) * size)], semaphore)

    others = pl.ds(0, (head_count - 1) * rows)

    def to_owners(chunk):
        if head_count > 1:
            wait_bytes(home.at[pl.ds(2 * chunk, 2), others], home_recv.at[chunk])

        def source(i):
            lane = (i % (pairs // 2)) * 2 * DH
            return home[2 * chunk + i // (pairs // 2), :, lane : lane + 2 * DH]

        pack(spread, source, send_buf, chunk)
        exchange(
            send_buf.at[chunk], recv_buf.at[chunk], block, there_send.at[chunk], there_recv.at[chunk]
        )

    def at_owner(chunk):
        wait_exchange(recv_buf.at[chunk], block, there_recv.at[chunk])

        def sink(i, value):
            owned[chunk * combos + 2 * i] = value[:, :DH]
            owned[chunk * combos + 2 * i + 1] = value[:, DH:]

        unpack(recv_buf, chunk, resort, sink)

    to_owners(0)
    to_owners(1)
    at_owner(0)

    for c in range(owned_count):
        mean_of = [
            jnp.sum(owned[i, c * CLUSTER : (c + 1) * CLUSTER, :].astype(F32), axis=0, keepdims=True)
            for i in range(combos)
        ]
        for i in range(combos):
            mean_msg[c * combos + i : c * combos + i + 1, :] = mean_of[i] / CLUSTER
    my_means = pl.ds(pl.multiple_of(me * mean_rows, mean_rows), mean_rows)
    mean_buf[my_means, :] = mean_msg[...].astype(BF16)

    @pl.loop(1, seq_count)
    def _(step):
        pltpu.make_async_remote_copy(
            src_ref=mean_buf.at[my_means],
            dst_ref=mean_buf.at[my_means],
            send_sem=mean_send,
            recv_sem=mean_recv,
            device_id={"seq": peer(step)},
            device_id_type=MESH,
        ).start()

    at_owner(1)
    wait_exchange(mean_buf, mean_rows, mean_recv)

    for g in range(mean_buf.shape[0] // side):
        moved = dot(tile_back[...], mean_buf[g * side : (g + 1) * side, :]).astype(BF16)
        for i in range(combos):
            means[i, g * TILE : (g + 1) * TILE, :] = moved[i * TILE : (i + 1) * TILE, :]

    @pl.loop(0, heads)
    def _(h):
        key_means = means[h, :mean_count, :]
        value_means = means[heads + h, :mean_count, :]
        for c in range(owned_count):
            part = pl.ds(c * CLUSTER, CLUSTER)
            keys = jnp.concatenate([owned[h, part, :], key_means], axis=0)
            values = jnp.concatenate([owned[heads + h, part, :], value_means], axis=0)
            queries = owned[combos + h, part, :]
            grads = owned[combos + heads + h, part, :]
            scores = dot(keys, queries, ((1,), (1,))) * scale
            scores = jnp.concatenate([scores[:CLUSTER] + hidden[c], scores[CLUSTER:]], axis=0)
            top = jnp.max(scores, axis=0, keepdims=True)
            powers = jnp.exp(scores - top)
            weights = powers * (1.0 / jnp.sum(powers, axis=0, keepdims=True))
            rounded = weights.astype(BF16)
            weight_grads = dot(values, grads, ((1,), (1,)))
            delta = jnp.sum(weights * weight_grads, axis=0, keepdims=True)
            steps = (weights * (weight_grads - delta)).astype(BF16)
            results[h, part, :] = dot(rounded, values, ((0,), (0,))).astype(BF16)
            results[heads + h, part, :] = (scale * dot(steps, keys, ((0,), (0,)))).astype(BF16)
            key_grads = scale * dot(steps, queries)
            value_grads = dot(rounded, grads)
            inner[h, part, :] = key_grads[:CLUSTER]
            inner[heads + h, part, :] = value_grads[:CLUSTER]
            if c == 0:
                mean_acc[h] = key_grads[CLUSTER:]
                mean_acc[heads + h] = value_grads[CLUSTER:]
            else:
                mean_acc[h] += key_grads[CLUSTER:]
                mean_acc[heads + h] += value_grads[CLUSTER:]

    for i in range(combos):
        grad_msg[pl.ds(i, mean_count, stride=combos), :] = mean_acc[i]
    exchange(grad_msg, grad_buf, mean_rows, grad_send, grad_recv)

    def result_pair(i):
        return jnp.concatenate([results[2 * i], results[2 * i + 1]], axis=1)

    pack(unsort, result_pair, back_send, 0)
    exchange(
        back_send.at[0], back_recv.at[0], block, back_send_sem.at[0], back_recv_sem.at[0]
    )

    wait_exchange(grad_buf, mean_rows, grad_recv)
    grad_sum[...] = jnp.sum(grad_buf[...].reshape(seq_count, mean_rows, DH), axis=0) / CLUSTER

    def final_pair(i):
        sides = []
        for j in (2 * i, 2 * i + 1):
            sides.append(
                jnp.concatenate(
                    [
                        inner[j, c * CLUSTER : (c + 1) * CLUSTER, :]
                        + grad_sum[c * combos + j : c * combos + j + 1, :]
                        for c in range(owned_count)
                    ],
                    axis=0,
                )
            )
        return jnp.concatenate(sides, axis=1).astype(BF16)

    pack(unsort, final_pair, back_send, 1)
    exchange(
        back_send.at[1], back_recv.at[1], block, back_send_sem.at[1], back_recv_sem.at[1]
    )

    outs = (out_a, out_q, out_k, out_v)

    def to_home(chunk):
        wait_exchange(back_recv.at[chunk], block, back_recv_sem.at[chunk])

        def sink(i, value):
            lane = (i % (pairs // 2)) * 2 * DH
            home_out[2 * chunk + i // (pairs // 2), :, lane : lane + 2 * DH] = value

        unpack(back_recv, chunk, gather, sink)
        for index in (2 * chunk, 2 * chunk + 1):
            out = outs[index]

            @pl.loop(1, head_count)
            def _(step, index=index, out=out):
                other = head_peer(step)
                pltpu.make_async_remote_copy(
                    src_ref=home_out.at[index, pl.ds(pl.multiple_of(other * rows, rows), rows)],
                    dst_ref=out.at[:, my_lanes],
                    send_sem=out_send.at[chunk],
                    recv_sem=out_recv.at[chunk],
                    device_id={"head": other},
                    device_id_type=MESH,
                ).start()

            out[:, my_lanes] = home_out[index, my_rows, :]

    to_home(0)
    to_home(1)

    if head_count > 1:
        for chunk in range(2):
            both = pl.ds(2 * chunk, 2)
            wait_bytes(home_out.at[both, others], out_recv.at[chunk])
            wait_bytes(home_out.at[both, others], out_send.at[chunk])
            wait_bytes(home.at[both, others], home_send.at[chunk])
    for chunk in range(2):
        wait_exchange(send_buf.at[chunk], block, there_send.at[chunk])
        wait_exchange(back_send.at[chunk], block, back_send_sem.at[chunk])
    wait_exchange(mean_buf, mean_rows, mean_send)
    wait_exchange(grad_msg, mean_rows, grad_send)


def per_device(queries, key_rows, value_rows, cotangent, cluster_of, order_tokens):
    seq_count = lax.axis_size("seq")
    head_count = lax.axis_size("head")
    rows, full = queries.shape
    group_rows = cluster_of.shape[0]
    width = full // head_count
    heads = width // DH
    combos = 2 * heads
    owned_count = group_rows // CLUSTER
    mean_slots = group_rows // seq_count
    capacity = mean_slots + mean_slots // 4
    slots = seq_count * capacity
    side = TILE * combos
    mean_rows = owned_count * combos
    mean_count = seq_count * owned_count
    mean_buf_rows = -(-seq_count * mean_rows // side) * side
    vmem = pltpu.VMEM
    scratch = [
        vmem((4, group_rows, width), BF16),
        vmem((combos // 2, slots, 2 * DH), BF16),
        vmem((2, slots * combos, DH), BF16),
        vmem((2, slots * combos, DH), BF16),
        vmem((2 * combos, group_rows, DH), BF16),
        vmem((mean_rows, DH), F32),
        vmem((mean_buf_rows, DH), BF16),
        vmem((combos, mean_buf_rows // combos, DH), BF16),
        vmem((combos, group_rows, DH), BF16),
        vmem((combos, group_rows, DH), F32),
        vmem((combos, mean_count, DH), F32),
        vmem((seq_count * mean_rows, DH), F32),
        vmem((seq_count * mean_rows, DH), F32),
        vmem((mean_rows, DH), F32),
        vmem((2, slots * combos, DH), BF16),
        vmem((2, slots * combos, DH), BF16),
        vmem((4, group_rows, width), BF16),
        vmem((slots, group_rows), BF16),
        vmem((group_rows, slots), BF16),
        vmem((slots, group_rows), BF16),
        vmem((group_rows, slots), BF16),
        vmem((side, side), BF16),
        vmem((side, side), BF16),
        vmem((owned_count, CLUSTER, CLUSTER), F32),
    ]
    dma = pltpu.SemaphoreType.DMA
    scratch += [dma((2,))] * 4 + [dma] * 4 + [dma((2,))] * 4
    in_vmem = pl.BlockSpec(memory_space=pltpu.VMEM)
    out = jax.ShapeDtypeStruct((rows, full), BF16)
    return pl.pallas_call(
        functools.partial(kernel, seq_count, head_count, heads, capacity),
        out_shape=(out,) * 4,
        in_specs=[in_vmem] * 6,
        out_specs=(in_vmem,) * 4,
        scratch_shapes=scratch,
        compiler_params=pltpu.CompilerParams(
            collective_id=0, has_side_effects=True, vmem_limit_bytes=48 * 1024 * 1024
        ),
    )(
        queries,
        key_rows,
        value_rows,
        cotangent,
        cluster_of.reshape(1, group_rows),
        order_tokens.reshape(1, group_rows),
    )


def solution(mesh):
    rows = P(("seq", "head"), None)
    return jax.shard_map(
        per_device,
        mesh=mesh,
        in_specs=(rows,) * 4 + (P("seq"),) * 2,
        out_specs=(rows,) * 4,
        check_vma=False,
    )
```

```python
import functools
import math

import jax
import jax.numpy as jnp
from jax import lax
from jax.experimental import pallas as pl
from jax.experimental.pallas import tpu as pltpu
from jax.sharding import PartitionSpec as P

DH = 128
CLUSTER = 256
MESH = pl.DeviceIdType.MESH
F32 = jnp.float32
BF16 = jnp.bfloat16

TILE = 32


def dot(a, b, dims=((1,), (0,))):
    return lax.dot_general(a, b, (dims, ((), ())), preferred_element_type=F32)


def as_column(row):
    return jnp.transpose(jnp.broadcast_to(row, (128, row.shape[1])))[:, :1]


def slot_vectors(group, rank_key, capacity):
    group_col, key_col = as_column(group), as_column(rank_key)
    same = group_col == group
    rank_col = jnp.sum(jnp.where(same & (rank_key < key_col), 1.0, 0.0), axis=1, keepdims=True)
    rank_row = jnp.sum(jnp.where(same & (key_col < rank_key), 1.0, 0.0), axis=0, keepdims=True)
    return group * capacity + rank_row, group_col * capacity + rank_col


def one_hot_rows(slot_row, count):
    slots = lax.broadcasted_iota(jnp.int32, (count, slot_row.shape[1]), 0).astype(F32)
    return jnp.where(slots == slot_row, 1.0, 0.0).astype(BF16)


def one_hot_columns(slot_col, count):
    slots = lax.broadcasted_iota(jnp.int32, (slot_col.shape[0], count), 1).astype(F32)
    return jnp.where(slots == slot_col, 1.0, 0.0).astype(BF16)


def kernel(
    seq_count, head_count, plane, capacity,
    q_ref, k_ref, v_ref, g_ref, cluster_ref, order_ref,
    out_a, out_q, out_k, out_v,
    home, mid, send_buf, recv_buf, owned, mean_msg, mean_buf, means,
    results, inner, mean_acc, grad_msg, grad_plane, grad_part, grad_line, grad_sum,
    back_send, back_recv, home_out,
    spread, gather, unsort, resort, tile_perm, tile_back, hidden,
    home_own, home_send, home_recv, there_send, there_recv,
    line_send, line_recv, plane_send, plane_recv,
    sum_plane_send, sum_plane_recv, sum_line_send, sum_line_recv,
    back_send_sem, back_recv_sem, out_send, out_recv,
):
    me = lax.axis_index("seq")
    my_head = lax.axis_index("head")
    rows, full = q_ref.shape
    width = full // head_count
    half = width // 2
    combos = 4 * half // DH
    group_rows = rows * head_count
    owned_count = group_rows // CLUSTER
    slots = seq_count * capacity
    block = capacity * combos
    mean_kinds = combos // 2
    mean_rows = owned_count * mean_kinds
    mean_count = seq_count * owned_count
    line = seq_count // plane
    my_line, my_plane = me // plane, lax.rem(me, plane)
    scale = DH ** (-0.5)

    def peer(step):
        return lax.rem(me + step, seq_count)

    def head_peer(step):
        return lax.rem(my_head + step, head_count)

    def line_peer(step):
        return lax.rem(my_line + step, line)

    def plane_peer(step):
        return lax.rem(my_plane + step, plane)

    def stretch(index, size):
        return pl.ds(pl.multiple_of(index * size, size), size)

    barrier = pltpu.get_barrier_semaphore()

    @pl.loop(1, head_count)
    def _(step):
        pl.semaphore_signal(
            barrier, inc=1, device_id={"head": head_peer(step)}, device_id_type=MESH
        )

    @pl.loop(1, seq_count)
    def _(step):
        pl.semaphore_signal(barrier, inc=1, device_id={"seq": peer(step)}, device_id_type=MESH)

    pl.semaphore_wait(barrier, head_count - 1 + seq_count - 1)

    def wait_bytes(ref, semaphore):
        pltpu.make_async_copy(ref, ref, semaphore).wait()

    def send(src, dst, send_sem, recv_sem, device):
        pltpu.make_async_remote_copy(
            src_ref=src,
            dst_ref=dst,
            send_sem=send_sem,
            recv_sem=recv_sem,
            device_id=device,
            device_id_type=MESH,
        ).start()

    my_rows = stretch(my_head, rows)
    others = pl.ds(0, (head_count - 1) * rows)

    def lanes(head, chunk):
        return pl.ds(pl.multiple_of(head * width + chunk * half, half), half)

    def to_heads(chunk):
        for index, ref in enumerate((k_ref, v_ref, q_ref, g_ref)):
            landing = home.at[chunk, index, my_rows]

            @pl.loop(1, head_count)
            def _(step, ref=ref, landing=landing):
                other = head_peer(step)
                send(
                    ref.at[:, lanes(other, chunk)],
                    landing,
                    home_send.at[chunk],
                    home_recv.at[chunk],
                    {"head": other},
                )

            pltpu.make_async_copy(
                ref.at[:, lanes(my_head, chunk)], landing, home_own.at[chunk]
            ).start()

    to_heads(0)

    target = (cluster_ref[...] // owned_count).astype(F32)
    position = lax.broadcasted_iota(jnp.int32, (1, group_rows), 1).astype(F32)
    row, column = slot_vectors(target, position, capacity)
    spread[...] = one_hot_rows(row, slots)
    gather[...] = one_hot_columns(column, slots)
    tokens_int = order_ref[...]
    tokens = tokens_int.astype(F32)
    row, column = slot_vectors((tokens_int // group_rows).astype(F32), tokens, capacity)
    unsort[...] = one_hot_rows(row, slots)
    resort[...] = one_hot_columns(column, slots)
    side = TILE * combos
    first = lax.broadcasted_iota(jnp.int32, (side, side), 0)
    second = lax.broadcasted_iota(jnp.int32, (side, side), 1)
    tile_perm[...] = jnp.where(
        second == (first % combos) * TILE + first // combos, 1.0, 0.0
    ).astype(BF16)
    tile_back[...] = jnp.where(
        first == (second % combos) * TILE + second // combos, 1.0, 0.0
    ).astype(BF16)
    for c in range(owned_count):
        part = tokens[:, c * CLUSTER : (c + 1) * CLUSTER]
        hidden[c] = jnp.where(as_column(part) <= part, 0.0, -jnp.inf)

    def pack(one_hot, source_ref, target_ref):
        @pl.loop(0, 4)
        def _(i):
            mid[i] = dot(one_hot[...], source_ref[i]).astype(BF16)

        @pl.loop(0, slots // (2 * TILE))
        def _(g):
            at = pl.multiple_of(g * 2 * TILE, 2 * TILE)
            parts = []
            for side_by_side in range(2):
                pieces = []
                for i in range(4):
                    piece = mid[i, pl.ds(at + side_by_side * TILE, TILE), :]
                    pieces += [piece[:, lane : lane + DH] for lane in range(0, half, DH)]
                parts.append(jnp.concatenate(pieces, axis=0))
            moved = dot(tile_perm[...], jnp.concatenate(parts, axis=1)).astype(BF16)
            to = pl.multiple_of(g * 2 * side, 2 * side)
            target_ref[pl.ds(to, side), :] = moved[:, :DH]
            target_ref[pl.ds(to + side, side), :] = moved[:, DH:]

    def unpack(source_ref, one_hot, target_ref):
        @pl.loop(0, slots // (2 * TILE))
        def _(g):
            at = pl.multiple_of(g * 2 * TILE, 2 * TILE)
            start = pl.multiple_of(g * 2 * side, 2 * side)
            both = jnp.concatenate(
                [source_ref[pl.ds(start, side), :], source_ref[pl.ds(start + side, side), :]],
                axis=1,
            )
            moved = dot(tile_back[...], both).astype(BF16)
            kinds = half // DH
            for side_by_side in range(2):
                part = moved[:, side_by_side * DH : (side_by_side + 1) * DH]
                for i in range(4):
                    pieces = [
                        part[(i * kinds + j) * TILE : (i * kinds + j + 1) * TILE]
                        for j in range(kinds)
                    ]
                    mid[i, pl.ds(at + side_by_side * TILE, TILE), :] = jnp.concatenate(
                        pieces, axis=1
                    )

        @pl.loop(0, 4)
        def _(i):
            target_ref[i] = dot(one_hot[...], mid[i]).astype(BF16)

    def exchange(source_ref, dest_ref, send_sem, recv_sem):
        mine = stretch(me, block)

        @pl.loop(1, seq_count)
        def _(step):
            other = peer(step)
            send(
                source_ref.at[stretch(other, block)],
                dest_ref.at[mine],
                send_sem,
                recv_sem,
                {"seq": other},
            )

        dest_ref[mine, :] = source_ref[mine, :]

    def wait_exchange(ref, semaphore):
        wait_bytes(ref.at[pl.ds(0, (seq_count - 1) * block)], semaphore)

    def to_owners(chunk):
        if head_count > 1:
            wait_bytes(home.at[chunk, :, others], home_recv.at[chunk])
        wait_bytes(home.at[chunk, :, pl.ds(0, rows)], home_own.at[chunk])
        pack(spread, home.at[chunk], send_buf.at[chunk])
        exchange(
            send_buf.at[chunk], recv_buf.at[chunk], there_send.at[chunk], there_recv.at[chunk]
        )

    def at_owner(chunk):
        wait_exchange(recv_buf.at[chunk], there_recv.at[chunk])
        unpack(recv_buf.at[chunk], resort, owned.at[chunk])

    def mean_gather(chunk):
        buf = mean_buf.at[chunk]
        for c in range(owned_count):
            for i in range(2):
                total = jnp.sum(
                    owned[chunk, i, c * CLUSTER : (c + 1) * CLUSTER, :].astype(F32),
                    axis=0,
                    keepdims=True,
                )
                for j in range(half // DH):
                    at = c * mean_kinds + i * (half // DH) + j
                    mean_msg[at : at + 1, :] = total[:, j * DH : (j + 1) * DH] / CLUSTER
        mine = stretch(my_plane * line + my_line, mean_rows)
        buf[mine, :] = mean_msg[...]

        @pl.loop(1, line)
        def _(step):
            send(
                buf.at[mine],
                buf.at[mine],
                line_send.at[chunk],
                line_recv.at[chunk],
                {"seq": line_peer(step) * plane + my_plane},
            )

        wait_bytes(buf.at[pl.ds(0, (line - 1) * mean_rows)], line_recv.at[chunk])
        my_part = stretch(my_plane, line * mean_rows)

        @pl.loop(1, plane)
        def _(step):
            send(
                buf.at[my_part],
                buf.at[my_part],
                plane_send.at[chunk],
                plane_recv.at[chunk],
                {"seq": my_line * plane + plane_peer(step)},
            )

        wait_bytes(buf.at[pl.ds(0, (plane - 1) * line * mean_rows)], plane_recv.at[chunk])
        for i in range(mean_kinds):
            means[i] = buf[pl.ds(i, mean_count, stride=mean_kinds), :].astype(BF16)

    def attend(chunk):
        kinds = half // DH

        @pl.loop(0, kinds)
        def _(h):
            lane = pl.ds(pl.multiple_of(h * DH, DH), DH)
            key_means = means[h]
            value_means = means[kinds + h]
            for c in range(owned_count):
                part = pl.ds(c * CLUSTER, CLUSTER)
                keys = jnp.concatenate([owned[chunk, 0, part, lane], key_means], axis=0)
                values = jnp.concatenate([owned[chunk, 1, part, lane], value_means], axis=0)
                queries = owned[chunk, 2, part, lane]
                grads = owned[chunk, 3, part, lane]
                scores = dot(keys, queries, ((1,), (1,))) * scale
                scores = jnp.concatenate([scores[:CLUSTER] + hidden[c], scores[CLUSTER:]], axis=0)
                top = jnp.max(scores, axis=0, keepdims=True)
                powers = jnp.exp(scores - top)
                weights = powers * (1.0 / jnp.sum(powers, axis=0, keepdims=True))
                rounded = weights.astype(BF16)
                weight_grads = dot(values, grads, ((1,), (1,)))
                delta = jnp.sum(weights * weight_grads, axis=0, keepdims=True)
                steps = (weights * (weight_grads - delta)).astype(BF16)
                results[0, part, lane] = dot(rounded, values, ((0,), (0,))).astype(BF16)
                results[1, part, lane] = (scale * dot(steps, keys, ((0,), (0,)))).astype(BF16)
                key_grads = scale * dot(steps, queries)
                value_grads = dot(rounded, grads)
                inner[0, part, lane] = key_grads[:CLUSTER]
                inner[1, part, lane] = value_grads[:CLUSTER]
                if c == 0:
                    mean_acc[h] = key_grads[CLUSTER:]
                    mean_acc[kinds + h] = value_grads[CLUSTER:]
                else:
                    mean_acc[h] += key_grads[CLUSTER:]
                    mean_acc[kinds + h] += value_grads[CLUSTER:]

    def grad_reduce(chunk):
        for i in range(mean_kinds):
            grad_msg[chunk, pl.ds(i, mean_count, stride=mean_kinds), :] = mean_acc[i]
        size = line * mean_rows
        mine = stretch(my_plane, size)

        @pl.loop(1, plane)
        def _(step):
            other = plane_peer(step)
            send(
                grad_msg.at[chunk, stretch(other, size)],
                grad_plane.at[chunk, mine],
                sum_plane_send.at[chunk],
                sum_plane_recv.at[chunk],
                {"seq": my_line * plane + other},
            )

        grad_plane[chunk, mine, :] = grad_msg[chunk, mine, :]
        wait_bytes(grad_plane.at[chunk, pl.ds(0, (plane - 1) * size)], sum_plane_recv.at[chunk])
        total = grad_plane[chunk, :size, :]
        for i in range(1, plane):
            total = total + grad_plane[chunk, i * size : (i + 1) * size, :]
        grad_part[chunk] = total
        my_slot = stretch(my_line, mean_rows)

        @pl.loop(1, line)
        def _(step):
            other = line_peer(step)
            send(
                grad_part.at[chunk, stretch(other, mean_rows)],
                grad_line.at[chunk, my_slot],
                sum_line_send.at[chunk],
                sum_line_recv.at[chunk],
                {"seq": other * plane + my_plane},
            )

        grad_line[chunk, my_slot, :] = grad_part[chunk, my_slot, :]
        wait_bytes(grad_line.at[chunk, pl.ds(0, (line - 1) * mean_rows)], sum_line_recv.at[chunk])
        total = grad_line[chunk, :mean_rows, :]
        for i in range(1, line):
            total = total + grad_line[chunk, i * mean_rows : (i + 1) * mean_rows, :]
        grad_sum[...] = total / CLUSTER

    def send_back(chunk):
        kinds = half // DH
        for i in range(2):
            for c in range(owned_count):
                part = slice(c * CLUSTER, (c + 1) * CLUSTER)
                for j in range(kinds):
                    lane = slice(j * DH, (j + 1) * DH)
                    at = c * mean_kinds + i * kinds + j
                    results[2 + i, part, lane] = (
                        inner[i, part, lane] + grad_sum[at : at + 1, :]
                    ).astype(BF16)
        pack(unsort, results, back_send.at[chunk])
        exchange(
            back_send.at[chunk],
            back_recv.at[chunk],
            back_send_sem.at[chunk],
            back_recv_sem.at[chunk],
        )

    def to_home(chunk):
        wait_exchange(back_recv.at[chunk], back_recv_sem.at[chunk])
        unpack(back_recv.at[chunk], gather, home_out.at[chunk])
        for index, out in enumerate((out_a, out_q, out_k, out_v)):

            @pl.loop(1, head_count)
            def _(step, index=index, out=out):
                other = head_peer(step)
                send(
                    home_out.at[chunk, index, stretch(other, rows)],
                    out.at[:, lanes(my_head, chunk)],
                    out_send.at[chunk],
                    out_recv.at[chunk],
                    {"head": other},
                )

            out[:, lanes(my_head, chunk)] = home_out[chunk, index, my_rows, :]

    to_owners(0)
    to_heads(1)
    to_owners(1)
    for chunk in range(2):
        at_owner(chunk)
        mean_gather(chunk)
        attend(chunk)
        grad_reduce(chunk)
        send_back(chunk)
    for chunk in range(2):
        to_home(chunk)

    for chunk in range(2):
        if head_count > 1:
            wait_bytes(home_out.at[chunk, :, others], out_recv.at[chunk])
            wait_bytes(home_out.at[chunk, :, others], out_send.at[chunk])
            wait_bytes(home.at[chunk, :, others], home_send.at[chunk])
        wait_exchange(send_buf.at[chunk], there_send.at[chunk])
        wait_exchange(back_send.at[chunk], back_send_sem.at[chunk])
        line_bytes = mean_buf.at[chunk, pl.ds(0, (line - 1) * mean_rows)]
        plane_bytes = mean_buf.at[chunk, pl.ds(0, (plane - 1) * line * mean_rows)]
        wait_bytes(line_bytes, line_send.at[chunk])
        wait_bytes(plane_bytes, plane_send.at[chunk])
        wait_bytes(plane_bytes, sum_plane_send.at[chunk])
        wait_bytes(line_bytes, sum_line_send.at[chunk])


def per_device(queries, key_rows, value_rows, cotangent, cluster_of, order_tokens):
    seq_count = lax.axis_size("seq")
    head_count = lax.axis_size("head")
    plane = math.isqrt(seq_count)
    rows, full = queries.shape
    group_rows = cluster_of.shape[0]
    width = full // head_count
    half = width // 2
    combos = 4 * half // DH
    owned_count = group_rows // CLUSTER
    mean_slots = group_rows // seq_count
    capacity = mean_slots + mean_slots // 4
    slots = seq_count * capacity
    side = TILE * combos
    mean_kinds = combos // 2
    mean_rows = owned_count * mean_kinds
    mean_count = seq_count * owned_count
    vmem = pltpu.VMEM
    scratch = [
        vmem((2, 4, group_rows, half), BF16),
        vmem((4, slots, half), BF16),
        vmem((2, slots * combos, DH), BF16),
        vmem((2, slots * combos, DH), BF16),
        vmem((2, 4, group_rows, half), BF16),
        vmem((mean_rows, DH), F32),
        vmem((2, seq_count * mean_rows, DH), F32),
        vmem((mean_kinds, mean_count, DH), BF16),
        vmem((4, group_rows, half), BF16),
        vmem((2, group_rows, half), F32),
        vmem((mean_kinds, mean_count, DH), F32),
        vmem((2, seq_count * mean_rows, DH), F32),
        vmem((2, seq_count * mean_rows, DH), F32),
        vmem((2, seq_count // plane * mean_rows, DH), F32),
        vmem((2, seq_count // plane * mean_rows, DH), F32),
        vmem((mean_rows, DH), F32),
        vmem((2, slots * combos, DH), BF16),
        vmem((2, slots * combos, DH), BF16),
        vmem((2, 4, group_rows, half), BF16),
        vmem((slots, group_rows), BF16),
        vmem((group_rows, slots), BF16),
        vmem((slots, group_rows), BF16),
        vmem((group_rows, slots), BF16),
        vmem((side, side), BF16),
        vmem((side, side), BF16),
        vmem((owned_count, CLUSTER, CLUSTER), F32),
    ]
    scratch += [pltpu.SemaphoreType.DMA((2,))] * 17
    anywhere = pl.BlockSpec(memory_space=pl.ANY)
    in_vmem = pl.BlockSpec(memory_space=pltpu.VMEM)
    out = jax.ShapeDtypeStruct((rows, full), BF16)
    return pl.pallas_call(
        functools.partial(kernel, seq_count, head_count, plane, capacity),
        out_shape=(out,) * 4,
        in_specs=[anywhere] * 4 + [in_vmem] * 2,
        out_specs=(in_vmem,) * 4,
        scratch_shapes=scratch,
        compiler_params=pltpu.CompilerParams(
            collective_id=0, has_side_effects=True, vmem_limit_bytes=48 * 1024 * 1024
        ),
    )(
        queries,
        key_rows,
        value_rows,
        cotangent,
        cluster_of.reshape(1, group_rows),
        order_tokens.reshape(1, group_rows),
    )


def solution(mesh):
    rows = P(("seq", "head"), None)
    return jax.shard_map(
        per_device,
        mesh=mesh,
        in_specs=(rows,) * 4 + (P("seq"),) * 2,
        out_specs=(rows,) * 4,
        check_vma=False,
    )
```

```python
import functools
import math

import jax
import jax.numpy as jnp
from jax import lax
from jax.experimental import pallas as pl
from jax.experimental.pallas import tpu as pltpu
from jax.sharding import PartitionSpec as P

DH = 128
CLUSTER = 256
MESH = pl.DeviceIdType.MESH
F32 = jnp.float32
BF16 = jnp.bfloat16

TILE = 32
PARTS = 4


def place_of(index, line, plane):
    at_line, at_plane = index // plane, index % plane
    pair = line // 2
    return (at_line % pair * 2 + at_line // pair) * plane + at_plane


def index_of(place, line, plane):
    at_line, at_plane = place // plane, place % plane
    return (at_line // 2 + at_line % 2 * (line // 2)) * plane + at_plane


def dot(a, b, dims=((1,), (0,))):
    return lax.dot_general(a, b, (dims, ((), ())), preferred_element_type=F32)


def as_column(row):
    return jnp.transpose(jnp.broadcast_to(row, (128, row.shape[1])))[:, :1]


def slot_vectors(group, rank_key, capacity):
    group_col, key_col = as_column(group), as_column(rank_key)
    same = group_col == group
    rank_col = jnp.sum(jnp.where(same & (rank_key < key_col), 1.0, 0.0), axis=1, keepdims=True)
    rank_row = jnp.sum(jnp.where(same & (key_col < rank_key), 1.0, 0.0), axis=0, keepdims=True)
    return group * capacity + rank_row, group_col * capacity + rank_col


def one_hot_rows(slot_row, count):
    slots = lax.broadcasted_iota(jnp.int32, (count, slot_row.shape[1]), 0).astype(F32)
    return jnp.where(slots == slot_row, 1.0, 0.0).astype(BF16)


def one_hot_columns(slot_col, count):
    slots = lax.broadcasted_iota(jnp.int32, (slot_col.shape[0], count), 1).astype(F32)
    return jnp.where(slots == slot_col, 1.0, 0.0).astype(BF16)


def kernel(
    seq_count, head_count, plane, capacity,
    q_ref, k_ref, v_ref, g_ref, cluster_ref, order_ref,
    out_ref,
    cluster_vec, order_vec, home, mid, send_buf, recv_buf, owned, mean_msg, mean_buf, means,
    results, inner, mean_acc, grad_msg, grad_plane, grad_part, grad_line, grad_sum,
    back_send, back_recv, home_out,
    spread, gather, unsort, resort, tile_perm, tile_back, hidden,
    home_own, home_send, home_recv, there_send, there_recv,
    back_send_sem, back_recv_sem, out_send, out_recv,
    table_sem, line_send, line_recv, plane_send, plane_recv,
    sum_plane_send, sum_plane_recv, sum_line_send, sum_line_recv, plane_ready,
):
    me = lax.axis_index("seq")
    my_head = lax.axis_index("head")
    rows, full = q_ref.shape
    width = full // head_count
    half = width // 2
    kinds = half // DH
    combos = 4 * kinds
    heads = width // DH
    group_rows = rows * head_count
    owned_count = group_rows // CLUSTER
    slots = seq_count * capacity
    part_slots = slots // PARTS
    part_peers = seq_count // PARTS
    block = capacity * combos
    side = TILE * combos
    mean_rows = owned_count * combos
    mean_count = seq_count * owned_count
    line = seq_count // plane
    my_line, my_plane = me // plane, lax.rem(me, plane)
    my_place = place_of(me, line, plane)
    my_part = my_place // part_peers
    scale = DH ** (-0.5)

    def head_peer(step):
        return lax.rem(my_head + step, head_count)

    def line_peer(step):
        return lax.rem(my_line + step, line)

    def plane_peer(step):
        return lax.rem(my_plane + step, plane)

    def stretch(index, size):
        return pl.ds(pl.multiple_of(index * size, size), size)

    def wait_bytes(ref, semaphore):
        pltpu.make_async_copy(ref, ref, semaphore).wait()

    def send(src, dst, send_sem, recv_sem, device):
        pltpu.make_async_remote_copy(
            src_ref=src,
            dst_ref=dst,
            send_sem=send_sem,
            recv_sem=recv_sem,
            device_id=device,
            device_id_type=MESH,
        ).start()

    barrier = pltpu.get_barrier_semaphore()

    def greet(semaphore, device):
        pl.semaphore_signal(semaphore, inc=1, device_id=device, device_id_type=MESH)

    @pl.loop(1, head_count)
    def _(step):
        greet(barrier, {"head": head_peer(step)})

    @pl.loop(1, line)
    def _(step):
        greet(barrier, {"seq": line_peer(step) * plane + my_plane})

    @pl.loop(1, plane)
    def _(step):
        greet(barrier, {"seq": my_line * plane + plane_peer(step)})

    table_copies = [
        pltpu.make_async_copy(cluster_ref, cluster_vec, table_sem.at[0]),
        pltpu.make_async_copy(order_ref, order_vec, table_sem.at[1]),
    ]
    for copy in table_copies:
        copy.start()

    pl.semaphore_wait(barrier, head_count - 1 + line - 1 + plane - 1)

    my_rows = stretch(my_head, rows)
    others = pl.ds(0, (head_count - 1) * rows)

    def lanes(head, i):
        return pl.ds(pl.multiple_of(head * width + (i % 2) * half, half), half)

    def to_heads(chunk, pairs=range(4)):
        for i in pairs:
            ref = ((k_ref, v_ref), (q_ref, g_ref))[chunk][i // 2]
            landing = home.at[chunk, i, my_rows]

            @pl.loop(1, head_count)
            def _(step, i=i, ref=ref, landing=landing):
                other = head_peer(step)
                send(
                    ref.at[:, lanes(other, i)],
                    landing,
                    home_send.at[chunk],
                    home_recv.at[chunk],
                    {"head": other},
                )

            pltpu.make_async_copy(
                ref.at[:, lanes(my_head, i)], landing, home_own.at[chunk]
            ).start()

    def from_heads(chunk):
        if head_count > 1:
            wait_bytes(home.at[chunk, :, others], home_recv.at[chunk])
        wait_bytes(home.at[chunk, :, pl.ds(0, rows)], home_own.at[chunk])

    to_heads(0)

    @pl.loop(1, plane)
    def _(step):
        greet(plane_ready, {"seq": my_line * plane + plane_peer(step)})

    for copy in table_copies:
        copy.wait()
    target = place_of(cluster_vec[...] // owned_count, line, plane).astype(F32)
    position = lax.broadcasted_iota(jnp.int32, (1, group_rows), 1).astype(F32)
    row, column = slot_vectors(target, position, capacity)
    spread[...] = one_hot_rows(row, slots)
    gather[...] = one_hot_columns(column, slots)
    tokens_int = order_vec[...]
    tokens = tokens_int.astype(F32)
    source = place_of(tokens_int // group_rows, line, plane).astype(F32)
    row, column = slot_vectors(source, tokens, capacity)
    unsort[...] = one_hot_rows(row, slots)
    resort[...] = one_hot_columns(column, slots)
    first = lax.broadcasted_iota(jnp.int32, (side, side), 0)
    second = lax.broadcasted_iota(jnp.int32, (side, side), 1)
    tile_perm[...] = jnp.where(
        second == (first % combos) * TILE + first // combos, 1.0, 0.0
    ).astype(BF16)
    tile_back[...] = jnp.where(
        first == (second % combos) * TILE + second // combos, 1.0, 0.0
    ).astype(BF16)
    for c in range(owned_count):
        piece = tokens[:, c * CLUSTER : (c + 1) * CLUSTER]
        hidden[c] = jnp.where(as_column(piece) <= piece, 0.0, -jnp.inf)
    if mean_buf.shape[0] > seq_count * mean_rows:
        mean_buf[...] = jnp.zeros_like(mean_buf)

    groups = part_slots // TILE

    def pack_part(one_hot, source_ref, buf, part):
        here = stretch(part, part_slots)
        hot = one_hot[here, :]
        pairs = [dot(hot, source_ref[i]).astype(BF16) for i in range(4)]
        tiles = []
        for g in range(groups):
            pieces = []
            for pair in pairs:
                piece = pair[g * TILE : (g + 1) * TILE]
                pieces += [piece[:, lane : lane + DH] for lane in range(0, half, DH)]
            tiles.append(jnp.concatenate(pieces, axis=0))
        moved = dot(tile_perm[...], jnp.concatenate(tiles, axis=1)).astype(BF16)
        for g in range(groups):
            buf[pl.ds(pl.multiple_of(part * part_slots * combos + g * side, side), side), :] = (
                moved[:, g * DH : (g + 1) * DH]
            )

    def send_part(buf, dest, part, send_sem, recv_sems, extra):
        mine = stretch(my_place, block)

        @pl.loop(0, part_peers)
        def _(step):
            place = part * part_peers + lax.rem(my_place + step * (plane + 1), part_peers)
            other = index_of(place, line, plane)

            @pl.when(place != my_place)
            def _():
                send(
                    buf.at[stretch(place, block)],
                    dest.at[mine],
                    send_sem,
                    recv_sems.at[my_part],
                    {"seq": other},
                )

            @pl.when(place == my_place)
            def _():
                dest[mine, :] = buf[mine, :]

            if extra is not None:
                extra(step)

    def pack_and_send(
        one_hot, source_ref, buf, dest, send_sem, recv_sems, first_step, last_step, extra=None
    ):
        @pl.loop(first_step, last_step)
        def _(step):
            part = lax.rem(my_part + step, PARTS)
            pack_part(one_hot, source_ref, buf, part)
            also = None
            if extra is not None:
                also = lambda inner_step: extra((step - first_step) * part_peers + inner_step)
            send_part(buf, dest, part, send_sem, recv_sems, also)

    def receive(buf, recv_sems):
        @pl.loop(0, PARTS)
        def _(step):
            part = lax.rem(my_part + PARTS - step, PARTS)
            whole = part_peers * block

            @pl.when(part != my_part)
            def _():
                wait_bytes(buf.at[pl.ds(0, whole)], recv_sems.at[part])

            @pl.when(part == my_part)
            def _():
                wait_bytes(buf.at[pl.ds(0, whole - block)], recv_sems.at[part])

            tiles = [
                buf[pl.ds(pl.multiple_of(part * whole + g * side, side), side), :]
                for g in range(groups)
            ]
            moved = dot(tile_back[...], jnp.concatenate(tiles, axis=1)).astype(BF16)
            for g in range(groups):
                column = moved[:, g * DH : (g + 1) * DH]
                to = pl.ds(pl.multiple_of(part * part_slots + g * TILE, TILE), TILE)
                for i in range(4):
                    pieces = [
                        column[(i * kinds + j) * TILE : (i * kinds + j + 1) * TILE]
                        for j in range(kinds)
                    ]
                    mid[i, to, :] = jnp.concatenate(pieces, axis=1)

    def wait_exchange(ref, semaphore):
        wait_bytes(ref.at[pl.ds(0, (seq_count - 1) * block)], semaphore)

    def to_owners(chunk, first_step, last_step):
        pack_and_send(
            spread,
            home.at[chunk],
            send_buf.at[chunk],
            recv_buf.at[chunk],
            there_send.at[chunk],
            there_recv.at[chunk],
            first_step,
            last_step,
        )

    def at_owner(chunk):
        receive(recv_buf.at[chunk], there_recv.at[chunk])

        @pl.loop(0, 4)
        def _(i):
            owned[chunk, i] = dot(resort[...], mid[i]).astype(BF16)

    my_means = stretch(my_plane * line + my_line, mean_rows)

    def mean_line():
        for c in range(owned_count):
            for i in range(4):
                total = jnp.sum(
                    owned[0, i, c * CLUSTER : (c + 1) * CLUSTER, :].astype(F32),
                    axis=0,
                    keepdims=True,
                )
                for j in range(kinds):
                    at = c * combos + i * kinds + j
                    mean_msg[at : at + 1, :] = total[:, j * DH : (j + 1) * DH] / CLUSTER
        mean_buf[my_means, :] = mean_msg[...].astype(BF16)

        @pl.loop(1, line)
        def _(step):
            send(
                mean_buf.at[my_means],
                mean_buf.at[my_means],
                line_send,
                line_recv,
                {"seq": line_peer(step) * plane + my_plane},
            )

    mean_line_bytes = mean_buf.at[pl.ds(0, (line - 1) * mean_rows)]
    mean_plane_bytes = mean_buf.at[pl.ds(0, (plane - 1) * line * mean_rows)]

    def mean_plane():
        wait_bytes(mean_line_bytes, line_recv)
        my_lines = stretch(my_plane, line * mean_rows)

        @pl.loop(1, plane)
        def _(step):
            send(
                mean_buf.at[my_lines],
                mean_buf.at[my_lines],
                plane_send,
                plane_recv,
                {"seq": my_line * plane + plane_peer(step)},
            )

    def mean_take():
        wait_bytes(mean_plane_bytes, plane_recv)
        for g in range(mean_buf.shape[0] // side):
            moved = dot(tile_back[...], mean_buf[g * side : (g + 1) * side, :]).astype(BF16)
            for i in range(combos):
                means[i, g * TILE : (g + 1) * TILE, :] = moved[i * TILE : (i + 1) * TILE, :]

    def attend():
        @pl.loop(0, heads)
        def _(h):
            pair = h // kinds
            lane = pl.ds(pl.multiple_of(lax.rem(h, kinds) * DH, DH), DH)
            key_means = means[h, :mean_count, :]
            value_means = means[heads + h, :mean_count, :]
            for c in range(owned_count):
                part = pl.ds(c * CLUSTER, CLUSTER)
                keys = jnp.concatenate([owned[0, pair, part, lane], key_means], axis=0)
                values = jnp.concatenate([owned[0, 2 + pair, part, lane], value_means], axis=0)
                queries = owned[1, pair, part, lane]
                grads = owned[1, 2 + pair, part, lane]
                scores = dot(keys, queries, ((1,), (1,))) * scale
                scores = jnp.concatenate([scores[:CLUSTER] + hidden[c], scores[CLUSTER:]], axis=0)
                top = jnp.max(scores, axis=0, keepdims=True)
                powers = jnp.exp(scores - top)
                weights = powers * (1.0 / jnp.sum(powers, axis=0, keepdims=True))
                rounded = weights.astype(BF16)
                weight_grads = dot(values, grads, ((1,), (1,)))
                delta = jnp.sum(weights * weight_grads, axis=0, keepdims=True)
                steps = (weights * (weight_grads - delta)).astype(BF16)
                results[pair, part, lane] = dot(rounded, values, ((0,), (0,))).astype(BF16)
                results[2 + pair, part, lane] = (scale * dot(steps, keys, ((0,), (0,)))).astype(
                    BF16
                )
                key_grads = scale * dot(steps, queries)
                value_grads = dot(rounded, grads)
                inner[pair, part, lane] = key_grads[:CLUSTER]
                inner[2 + pair, part, lane] = value_grads[:CLUSTER]
                if c == 0:
                    mean_acc[h] = key_grads[CLUSTER:]
                    mean_acc[heads + h] = value_grads[CLUSTER:]
                else:
                    mean_acc[h] += key_grads[CLUSTER:]
                    mean_acc[heads + h] += value_grads[CLUSTER:]

    plane_size = line * mean_rows

    def grad_pack():
        for i in range(combos):
            grad_msg[pl.ds(i, mean_count, stride=combos), :] = mean_acc[i]
        mine = stretch(my_plane, plane_size)
        grad_plane[mine, :] = grad_msg[mine, :]

    pieces = (plane - 1) * line
    piece_steps = 2 * part_peers
    pieces_per_step = -(-pieces // piece_steps)

    def grad_to_plane(step):
        for i in range(pieces_per_step):
            number = step * pieces_per_step + i

            @pl.when(number < pieces)
            def _(number=number):
                other = plane_peer(number // line + 1)
                at_line = number % line
                send(
                    grad_msg.at[stretch(other * line + at_line, mean_rows)],
                    grad_plane.at[stretch(my_plane * line + at_line, mean_rows)],
                    sum_plane_send,
                    sum_plane_recv,
                    {"seq": my_line * plane + other},
                )

    grad_plane_bytes = grad_plane.at[pl.ds(0, (plane - 1) * plane_size)]
    grad_line_bytes = grad_line.at[pl.ds(0, (line - 1) * mean_rows)]

    def grad_to_line():
        wait_bytes(grad_plane_bytes, sum_plane_recv)
        total = grad_plane[:plane_size, :]
        for i in range(1, plane):
            total = total + grad_plane[i * plane_size : (i + 1) * plane_size, :]
        grad_part[...] = total
        mine = stretch(my_line, mean_rows)

        @pl.loop(1, line)
        def _(step):
            other = line_peer(step)
            send(
                grad_part.at[stretch(other, mean_rows)],
                grad_line.at[mine],
                sum_line_send,
                sum_line_recv,
                {"seq": other * plane + my_plane},
            )

        grad_line[mine, :] = grad_part[mine, :]

    def grad_finish():
        wait_bytes(grad_line_bytes, sum_line_recv)
        total = grad_line[:mean_rows, :]
        for i in range(1, line):
            total = total + grad_line[i * mean_rows : (i + 1) * mean_rows, :]
        grad_sum[...] = total / CLUSTER
        for i in range(4):
            for c in range(owned_count):
                part = slice(c * CLUSTER, (c + 1) * CLUSTER)
                for j in range(kinds):
                    lane = slice(j * DH, (j + 1) * DH)
                    at = c * combos + i * kinds + j
                    results[i, part, lane] = (
                        inner[i, part, lane] + grad_sum[at : at + 1, :]
                    ).astype(BF16)

    def send_back(chunk, first_step, last_step, extra=None):
        pack_and_send(
            unsort,
            results,
            back_send.at[chunk],
            back_recv.at[chunk],
            back_send_sem.at[chunk],
            back_recv_sem.at[chunk],
            first_step,
            last_step,
            extra,
        )

    def to_home(chunk):
        receive(back_recv.at[chunk], back_recv_sem.at[chunk])
        for i in range(4):
            home_out[chunk, i] = dot(gather[...], mid[i]).astype(BF16)
            place = out_ref.at[2 * chunk + i // 2, :, lanes(my_head, i)]

            @pl.loop(1, head_count)
            def _(step, i=i, place=place):
                other = head_peer(step)
                send(
                    home_out.at[chunk, i, stretch(other, rows)],
                    place,
                    out_send.at[chunk],
                    out_recv.at[chunk],
                    {"head": other},
                )

            place[...] = home_out[chunk, i, my_rows, :]

    from_heads(0)
    pl.semaphore_wait(plane_ready, plane - 1)
    to_owners(0, 0, 2)
    to_heads(1, range(2))
    to_owners(0, 2, PARTS)
    to_heads(1, range(2, 4))
    from_heads(1)
    to_owners(1, 0, 2)
    at_owner(0)
    mean_line()
    to_owners(1, 2, 3)
    mean_plane()
    to_owners(1, 3, PARTS)
    mean_take()
    at_owner(1)
    attend()
    grad_pack()
    send_back(0, 0, 2, grad_to_plane)
    send_back(0, 2, 3)
    grad_to_line()
    send_back(0, 3, PARTS)
    grad_finish()
    send_back(1, 0, 2)
    to_home(0)
    send_back(1, 2, PARTS)
    to_home(1)

    for chunk in range(2):
        if head_count > 1:
            wait_bytes(home_out.at[chunk, :, others], out_recv.at[chunk])
            wait_bytes(home_out.at[chunk, :, others], out_send.at[chunk])
            wait_bytes(home.at[chunk, :, others], home_send.at[chunk])
        wait_exchange(send_buf.at[chunk], there_send.at[chunk])
        wait_exchange(back_send.at[chunk], back_send_sem.at[chunk])
    wait_bytes(mean_line_bytes, line_send)
    wait_bytes(mean_plane_bytes, plane_send)
    wait_bytes(grad_plane_bytes, sum_plane_send)
    wait_bytes(grad_line_bytes, sum_line_send)


def per_device(queries, key_rows, value_rows, cotangent, cluster_of, order_tokens):
    seq_count = lax.axis_size("seq")
    head_count = lax.axis_size("head")
    plane = math.isqrt(seq_count)
    rows, full = queries.shape
    group_rows = cluster_of.shape[0]
    width = full // head_count
    half = width // 2
    combos = 4 * half // DH
    owned_count = group_rows // CLUSTER
    mean_slots = group_rows // seq_count
    capacity = mean_slots + mean_slots // 4
    slots = seq_count * capacity
    side = TILE * combos
    mean_rows = owned_count * combos
    mean_count = seq_count * owned_count
    mean_buf_rows = -(-seq_count * mean_rows // side) * side
    line_rows = seq_count // plane * mean_rows
    vmem = pltpu.VMEM
    scratch = [
        vmem((1, group_rows), jnp.int32),
        vmem((1, group_rows), jnp.int32),
        vmem((2, 4, group_rows, half), BF16),
        vmem((4, slots, half), BF16),
        vmem((2, slots * combos, DH), BF16),
        vmem((2, slots * combos, DH), BF16),
        vmem((2, 4, group_rows, half), BF16),
        vmem((mean_rows, DH), F32),
        vmem((mean_buf_rows, DH), BF16),
        vmem((combos, mean_buf_rows // combos, DH), BF16),
        vmem((4, group_rows, half), BF16),
        vmem((4, group_rows, half), F32),
        vmem((combos, mean_count, DH), F32),
        vmem((seq_count * mean_rows, DH), F32),
        vmem((seq_count * mean_rows, DH), F32),
        vmem((line_rows, DH), F32),
        vmem((line_rows, DH), F32),
        vmem((mean_rows, DH), F32),
        vmem((2, slots * combos, DH), BF16),
        vmem((2, slots * combos, DH), BF16),
        vmem((2, 4, group_rows, half), BF16),
        vmem((slots, group_rows), BF16),
        vmem((group_rows, slots), BF16),
        vmem((slots, group_rows), BF16),
        vmem((group_rows, slots), BF16),
        vmem((side, side), BF16),
        vmem((side, side), BF16),
        vmem((owned_count, CLUSTER, CLUSTER), F32),
    ]
    dma = pltpu.SemaphoreType.DMA
    by_chunk, by_part = dma((2,)), dma((2, PARTS))
    scratch += [by_chunk] * 4 + [by_part, by_chunk, by_part] + [by_chunk] * 3 + [dma] * 8
    scratch += [pltpu.SemaphoreType.REGULAR]
    in_hbm = pl.BlockSpec(memory_space=pltpu.HBM)
    in_vmem = pl.BlockSpec(memory_space=pltpu.VMEM)
    staged = pl.pallas_call(
        functools.partial(kernel, seq_count, head_count, plane, capacity),
        out_shape=jax.ShapeDtypeStruct((4, rows, full), BF16),
        in_specs=[in_hbm] * 6,
        out_specs=in_vmem,
        scratch_shapes=scratch,
        compiler_params=pltpu.CompilerParams(
            collective_id=0, has_side_effects=True, vmem_limit_bytes=63 * 1024 * 1024
        ),
    )(
        queries,
        key_rows,
        value_rows,
        cotangent,
        cluster_of.reshape(1, group_rows),
        order_tokens.reshape(1, group_rows),
    )
    return tuple(staged[i] for i in range(4))


def solution(mesh):
    rows = P(("seq", "head"), None)
    return jax.shard_map(
        per_device,
        mesh=mesh,
        in_specs=(rows,) * 4 + (P("seq"),) * 2,
        out_specs=(rows,) * 4,
        check_vma=False,
    )
```

```python
import functools
import math

import jax
import jax.numpy as jnp
from jax import lax
from jax.experimental import pallas as pl
from jax.experimental.pallas import tpu as pltpu
from jax.sharding import PartitionSpec as P

DH = 128
CLUSTER = 256
MESH = pl.DeviceIdType.MESH
F32 = jnp.float32
BF16 = jnp.bfloat16

TILE = 32
PARTS = 4


def place_of(index, line, plane):
    at_line, at_plane = index // plane, index % plane
    pair = line // 2
    return (at_line % pair * 2 + at_line // pair) * plane + at_plane


def index_of(place, line, plane):
    at_line, at_plane = place // plane, place % plane
    return (at_line // 2 + at_line % 2 * (line // 2)) * plane + at_plane


def dot(a, b, dims=((1,), (0,))):
    return lax.dot_general(a, b, (dims, ((), ())), preferred_element_type=F32)


def as_column(row):
    return jnp.transpose(jnp.broadcast_to(row, (128, row.shape[1])))[:, :1]


def slot_vectors(group, rank_key, capacity, early, groups):
    group_col, key_col = as_column(group), as_column(rank_key)
    same = group_col == group
    rank_col = jnp.sum(jnp.where(same & (rank_key < key_col), 1.0, 0.0), axis=1, keepdims=True)
    rank_row = jnp.sum(jnp.where(same & (key_col < rank_key), 1.0, 0.0), axis=0, keepdims=True)

    def split(group, rank):
        late = early * groups + group * (capacity - early) + rank - early
        return jnp.where(rank < early, group * early + rank, late)

    return (
        group * capacity + rank_row,
        group_col * capacity + rank_col,
        split(group, rank_row),
        split(group_col, rank_col),
    )


def one_hot_rows(slot_row, count):
    slots = lax.broadcasted_iota(jnp.int32, (count, slot_row.shape[1]), 0).astype(F32)
    return jnp.where(slots == slot_row, 1.0, 0.0).astype(BF16)


def one_hot_columns(slot_col, count):
    slots = lax.broadcasted_iota(jnp.int32, (slot_col.shape[0], count), 1).astype(F32)
    return jnp.where(slots == slot_col, 1.0, 0.0).astype(BF16)


def kernel(
    seq_count, head_count, plane, capacity,
    q_ref, k_ref, v_ref, g_ref, cluster_ref, order_ref,
    out_ref,
    cluster_vec, order_vec, home, mid, send_buf, recv_buf, owned, asked, mean_msg, mean_buf, means,
    answers, results, inner, mean_acc, grad_msg, grad_plane, grad_part, grad_line, grad_sum,
    back_send, back_recv, home_out,
    spread, gather, spread_split, gather_split, unsort, resort, tile_perm, tile_back, hidden,
    home_own, home_send, home_recv, there_send, there_recv,
    back_send_sem, back_recv_sem, out_send, out_recv,
    table_sem, line_send, line_recv, plane_send, plane_recv,
    sum_plane_send, sum_plane_recv, sum_line_send, sum_line_recv, plane_ready,
):
    me = lax.axis_index("seq")
    my_head = lax.axis_index("head")
    rows, full = q_ref.shape
    width = full // head_count
    half = width // 2
    kinds = half // DH
    combos = 4 * kinds
    heads = width // DH
    group_rows = rows * head_count
    owned_count = group_rows // CLUSTER
    slots = seq_count * capacity
    early = capacity * 3 // 5
    part_peers = seq_count // PARTS
    side = TILE * combos
    mean_rows = owned_count * combos
    mean_count = seq_count * owned_count
    line = seq_count // plane
    my_line, my_plane = me // plane, lax.rem(me, plane)
    my_place = place_of(me, line, plane)
    my_part = my_place // part_peers
    scale = DH ** (-0.5)

    def head_peer(step):
        return lax.rem(my_head + step, head_count)

    def line_peer(step):
        return lax.rem(my_line + step, line)

    def plane_peer(step):
        return lax.rem(my_plane + step, plane)

    def stretch(index, size):
        return pl.ds(pl.multiple_of(index * size, size), size)

    def wait_bytes(ref, semaphore):
        pltpu.make_async_copy(ref, ref, semaphore).wait()

    def send(src, dst, send_sem, recv_sem, device):
        pltpu.make_async_remote_copy(
            src_ref=src,
            dst_ref=dst,
            send_sem=send_sem,
            recv_sem=recv_sem,
            device_id=device,
            device_id_type=MESH,
        ).start()

    barrier = pltpu.get_barrier_semaphore()

    def greet(semaphore, device):
        pl.semaphore_signal(semaphore, inc=1, device_id=device, device_id_type=MESH)

    @pl.loop(1, head_count)
    def _(step):
        greet(barrier, {"head": head_peer(step)})

    @pl.loop(1, line)
    def _(step):
        greet(barrier, {"seq": line_peer(step) * plane + my_plane})

    @pl.loop(1, plane)
    def _(step):
        greet(barrier, {"seq": my_line * plane + plane_peer(step)})

    table_copies = [
        pltpu.make_async_copy(cluster_ref, cluster_vec, table_sem.at[0]),
        pltpu.make_async_copy(order_ref, order_vec, table_sem.at[1]),
    ]
    for copy in table_copies:
        copy.start()

    pl.semaphore_wait(barrier, head_count - 1 + line - 1 + plane - 1)

    my_rows = stretch(my_head, rows)
    others = pl.ds(0, (head_count - 1) * rows)

    def lanes(head, i):
        return pl.ds(pl.multiple_of(head * width + (i % 2) * half, half), half)

    def to_heads(chunk, pairs=range(4)):
        for i in pairs:
            ref = ((k_ref, v_ref), (q_ref, g_ref))[chunk][i // 2]
            landing = home.at[chunk, i, my_rows]

            @pl.loop(1, head_count)
            def _(step, i=i, ref=ref, landing=landing):
                other = head_peer(step)
                send(
                    ref.at[:, lanes(other, i)],
                    landing,
                    home_send.at[chunk],
                    home_recv.at[chunk],
                    {"head": other},
                )

            pltpu.make_async_copy(
                ref.at[:, lanes(my_head, i)], landing, home_own.at[chunk]
            ).start()

    def from_heads(chunk):
        if head_count > 1:
            wait_bytes(home.at[chunk, :, others], home_recv.at[chunk])
        wait_bytes(home.at[chunk, :, pl.ds(0, rows)], home_own.at[chunk])

    to_heads(0)

    @pl.loop(1, plane)
    def _(step):
        greet(plane_ready, {"seq": my_line * plane + plane_peer(step)})

    for copy in table_copies:
        copy.wait()
    target = place_of(cluster_vec[...] // owned_count, line, plane).astype(F32)
    position = lax.broadcasted_iota(jnp.int32, (1, group_rows), 1).astype(F32)
    row, column, split_row, split_column = slot_vectors(
        target, position, capacity, early, seq_count
    )
    spread[...] = one_hot_rows(row, slots)
    gather[...] = one_hot_columns(column, slots)
    spread_split[...] = one_hot_rows(split_row, slots)
    gather_split[...] = one_hot_columns(split_column, slots)
    tokens_int = order_vec[...]
    tokens = tokens_int.astype(F32)
    source = place_of(tokens_int // group_rows, line, plane).astype(F32)
    row, column, _, split_column = slot_vectors(source, tokens, capacity, early, seq_count)
    unsort[...] = one_hot_rows(row, slots)
    resort[...] = one_hot_columns(column, slots)
    token_column = as_column(tokens)
    cell_column = (
        1 + lax.broadcasted_iota(jnp.int32, (group_rows, 1), 0) // CLUSTER
    ).astype(F32)
    slot_numbers = lax.broadcasted_iota(jnp.int32, (group_rows, slots), 1).astype(F32)
    held = slot_numbers == split_column
    slot_token = jnp.sum(jnp.where(held, token_column, 0.0), axis=0, keepdims=True)
    slot_cell = jnp.sum(jnp.where(held, cell_column, 0.0), axis=0, keepdims=True)
    hidden[...] = jnp.where(
        (cell_column == slot_cell) & (token_column <= slot_token), 0.0, -jnp.inf
    )
    first = lax.broadcasted_iota(jnp.int32, (side, side), 0)
    second = lax.broadcasted_iota(jnp.int32, (side, side), 1)
    tile_perm[...] = jnp.where(
        second == (first % combos) * TILE + first // combos, 1.0, 0.0
    ).astype(BF16)
    tile_back[...] = jnp.where(
        first == (second % combos) * TILE + second // combos, 1.0, 0.0
    ).astype(BF16)
    if mean_buf.shape[0] > seq_count * mean_rows:
        mean_buf[...] = jnp.zeros_like(mean_buf)

    def flow(size, base, one_hot, source_ref, out_buf, in_buf, send_sem, recv_sems):
        count = size * seq_count
        here = pl.ds(base * combos, count * combos)
        return (
            size, base, one_hot, source_ref, out_buf.at[here], in_buf.at[here], send_sem, recv_sems
        )

    def pack_part(stream, part):
        size, base, one_hot, source_ref, buf, _, _, _ = stream
        part_slots = size * part_peers
        start = pl.multiple_of(base + part * part_slots, TILE)
        if one_hot is None:
            pairs = [source_ref[i, pl.ds(start, part_slots), :] for i in range(4)]
        else:
            hot = one_hot[pl.ds(start, part_slots), :]
            pairs = [dot(hot, source_ref[i]).astype(BF16) for i in range(4)]
        groups = part_slots // TILE
        tiles = []
        for g in range(groups):
            pieces = []
            for pair in pairs:
                piece = pair[g * TILE : (g + 1) * TILE]
                pieces += [piece[:, lane : lane + DH] for lane in range(0, half, DH)]
            tiles.append(jnp.concatenate(pieces, axis=0))
        moved = dot(tile_perm[...], jnp.concatenate(tiles, axis=1)).astype(BF16)
        for g in range(groups):
            buf[pl.ds(pl.multiple_of(part * part_slots * combos + g * side, side), side), :] = (
                moved[:, g * DH : (g + 1) * DH]
            )

    def send_part(stream, part, extra):
        size, _, _, _, buf, dest, send_sem, recv_sems = stream
        block = size * combos
        mine = stretch(my_place, block)

        @pl.loop(0, part_peers)
        def _(step):
            place = part * part_peers + lax.rem(my_place + step * (plane + 1), part_peers)
            other = index_of(place, line, plane)

            @pl.when(place != my_place)
            def _():
                send(
                    buf.at[stretch(place, block)],
                    dest.at[mine],
                    send_sem,
                    recv_sems.at[my_part],
                    {"seq": other},
                )

            @pl.when(place == my_place)
            def _():
                dest[mine, :] = buf[mine, :]

            if extra is not None:
                extra(step)

    def pack_and_send(stream, first_step, last_step, extra=None):
        @pl.loop(first_step, last_step)
        def _(step):
            part = lax.rem(my_part + step, PARTS)
            pack_part(stream, part)
            also = None
            if extra is not None:
                also = lambda inner_step: extra((step - first_step) * part_peers + inner_step)
            send_part(stream, part, also)

    def receive(stream, target_ref):
        size, base, _, _, _, buf, _, recv_sems = stream
        block = size * combos
        part_slots = size * part_peers
        groups = part_slots // TILE
        whole = part_peers * block

        @pl.loop(0, PARTS)
        def _(step):
            part = lax.rem(my_part + PARTS - step, PARTS)

            @pl.when(part != my_part)
            def _():
                wait_bytes(buf.at[pl.ds(0, whole)], recv_sems.at[part])

            @pl.when(part == my_part)
            def _():
                wait_bytes(buf.at[pl.ds(0, whole - block)], recv_sems.at[part])

            tiles = [
                buf[pl.ds(pl.multiple_of(part * whole + g * side, side), side), :]
                for g in range(groups)
            ]
            moved = dot(tile_back[...], jnp.concatenate(tiles, axis=1)).astype(BF16)
            for g in range(groups):
                column = moved[:, g * DH : (g + 1) * DH]
                to = pl.ds(pl.multiple_of(base + part * part_slots + g * TILE, TILE), TILE)
                for i in range(4):
                    pieces = [
                        column[(i * kinds + j) * TILE : (i * kinds + j + 1) * TILE]
                        for j in range(kinds)
                    ]
                    target_ref[i, to, :] = jnp.concatenate(pieces, axis=1)

    def flows(chunk, one_hot, source_ref, split_hot, split_source, out_buf, in_buf, sends, recvs):
        first, second = out_buf.at[chunk], in_buf.at[chunk]
        late = early * seq_count
        if one_hot is not None:
            return flow(
                capacity, 0, one_hot, source_ref, first, second, sends.at[0], recvs.at[0]
            )
        return (
            flow(early, 0, split_hot, split_source, first, second, sends.at[1], recvs.at[1]),
            flow(
                capacity - early, late, split_hot, split_source, first, second,
                sends.at[2], recvs.at[2],
            ),
        )

    keys_flow = flows(
        0, spread, home.at[0], None, None, send_buf, recv_buf, there_send, there_recv
    )
    query_flows = flows(
        1, None, None, spread_split, home.at[1], send_buf, recv_buf, there_send, there_recv
    )
    answer_flows = flows(
        0, None, None, None, answers, back_send, back_recv, back_send_sem, back_recv_sem
    )
    grads_flow = flows(
        1, unsort, results, None, None, back_send, back_recv, back_send_sem, back_recv_sem
    )

    def wait_sent(stream):
        size, _, _, _, buf, _, send_sem, _ = stream
        wait_bytes(buf.at[pl.ds(0, (seq_count - 1) * size * combos)], send_sem)

    def keys_arrive():
        receive(keys_flow, mid)

        @pl.loop(0, 4)
        def _(i):
            owned[i] = dot(resort[...], mid[i]).astype(BF16)

    my_means = stretch(my_plane * line + my_line, mean_rows)

    def mean_line():
        for c in range(owned_count):
            for i in range(4):
                total = jnp.sum(
                    owned[i, c * CLUSTER : (c + 1) * CLUSTER, :].astype(F32),
                    axis=0,
                    keepdims=True,
                )
                for j in range(kinds):
                    at = c * combos + i * kinds + j
                    mean_msg[at : at + 1, :] = total[:, j * DH : (j + 1) * DH] / CLUSTER
        mean_buf[my_means, :] = mean_msg[...].astype(BF16)

        @pl.loop(1, line)
        def _(step):
            send(
                mean_buf.at[my_means],
                mean_buf.at[my_means],
                line_send,
                line_recv,
                {"seq": line_peer(step) * plane + my_plane},
            )

    mean_line_bytes = mean_buf.at[pl.ds(0, (line - 1) * mean_rows)]
    mean_plane_bytes = mean_buf.at[pl.ds(0, (plane - 1) * line * mean_rows)]

    def mean_plane():
        wait_bytes(mean_line_bytes, line_recv)
        my_lines = stretch(my_plane, line * mean_rows)

        @pl.loop(1, plane)
        def _(step):
            send(
                mean_buf.at[my_lines],
                mean_buf.at[my_lines],
                plane_send,
                plane_recv,
                {"seq": my_line * plane + plane_peer(step)},
            )

    def mean_take():
        wait_bytes(mean_plane_bytes, plane_recv)
        for g in range(mean_buf.shape[0] // side):
            moved = dot(tile_back[...], mean_buf[g * side : (g + 1) * side, :]).astype(BF16)
            for i in range(combos):
                means[i, g * TILE : (g + 1) * TILE, :] = moved[i * TILE : (i + 1) * TILE, :]

    def attend(which):
        size, base = query_flows[which][:2]
        part = pl.ds(base, size * seq_count)

        @pl.loop(0, heads)
        def _(h):
            pair = h // kinds
            lane = pl.ds(pl.multiple_of(lax.rem(h, kinds) * DH, DH), DH)
            keys = jnp.concatenate([owned[pair, :, lane], means[h, :mean_count, :]], axis=0)
            values = jnp.concatenate(
                [owned[2 + pair, :, lane], means[heads + h, :mean_count, :]], axis=0
            )
            queries = asked[pair, part, lane]
            grads = asked[2 + pair, part, lane]
            scores = dot(keys, queries, ((1,), (1,))) * scale
            scores = jnp.concatenate(
                [scores[:group_rows] + hidden[:, part], scores[group_rows:]], axis=0
            )
            top = jnp.max(scores, axis=0, keepdims=True)
            powers = jnp.exp(scores - top)
            weights = powers * (1.0 / jnp.sum(powers, axis=0, keepdims=True))
            rounded = weights.astype(BF16)
            weight_grads = dot(values, grads, ((1,), (1,)))
            delta = jnp.sum(weights * weight_grads, axis=0, keepdims=True)
            steps = (weights * (weight_grads - delta)).astype(BF16)
            answers[pair, part, lane] = dot(rounded, values, ((0,), (0,))).astype(BF16)
            answers[2 + pair, part, lane] = (scale * dot(steps, keys, ((0,), (0,)))).astype(BF16)
            key_grads = scale * dot(steps, queries)
            value_grads = dot(rounded, grads)
            if which == 0:
                inner[pair, :, lane] = key_grads[:group_rows]
                inner[2 + pair, :, lane] = value_grads[:group_rows]
                mean_acc[h] = key_grads[group_rows:]
                mean_acc[heads + h] = value_grads[group_rows:]
            else:
                inner[pair, :, lane] += key_grads[:group_rows]
                inner[2 + pair, :, lane] += value_grads[:group_rows]
                mean_acc[h] += key_grads[group_rows:]
                mean_acc[heads + h] += value_grads[group_rows:]

    plane_size = line * mean_rows

    def grad_pack():
        for i in range(combos):
            grad_msg[pl.ds(i, mean_count, stride=combos), :] = mean_acc[i]
        mine = stretch(my_plane, plane_size)
        grad_plane[mine, :] = grad_msg[mine, :]

    pieces = (plane - 1) * line
    piece_steps = 2 * part_peers
    pieces_per_step = -(-pieces // piece_steps)

    def grad_to_plane(step):
        for i in range(pieces_per_step):
            number = step * pieces_per_step + i

            @pl.when(number < pieces)
            def _(number=number):
                other = plane_peer(number // line + 1)
                at_line = number % line
                send(
                    grad_msg.at[stretch(other * line + at_line, mean_rows)],
                    grad_plane.at[stretch(my_plane * line + at_line, mean_rows)],
                    sum_plane_send,
                    sum_plane_recv,
                    {"seq": my_line * plane + other},
                )

    grad_plane_bytes = grad_plane.at[pl.ds(0, (plane - 1) * plane_size)]
    grad_line_bytes = grad_line.at[pl.ds(0, (line - 1) * mean_rows)]

    def grad_to_line():
        wait_bytes(grad_plane_bytes, sum_plane_recv)
        total = grad_plane[:plane_size, :]
        for i in range(1, plane):
            total = total + grad_plane[i * plane_size : (i + 1) * plane_size, :]
        grad_part[...] = total
        mine = stretch(my_line, mean_rows)

        @pl.loop(1, line)
        def _(step):
            other = line_peer(step)
            send(
                grad_part.at[stretch(other, mean_rows)],
                grad_line.at[mine],
                sum_line_send,
                sum_line_recv,
                {"seq": other * plane + my_plane},
            )

        grad_line[mine, :] = grad_part[mine, :]

    def grad_finish():
        wait_bytes(grad_line_bytes, sum_line_recv)
        total = grad_line[:mean_rows, :]
        for i in range(1, line):
            total = total + grad_line[i * mean_rows : (i + 1) * mean_rows, :]
        grad_sum[...] = total / CLUSTER
        for i in range(4):
            for c in range(owned_count):
                part = slice(c * CLUSTER, (c + 1) * CLUSTER)
                for j in range(kinds):
                    lane = slice(j * DH, (j + 1) * DH)
                    at = c * combos + i * kinds + j
                    results[i, part, lane] = (
                        inner[i, part, lane] + grad_sum[at : at + 1, :]
                    ).astype(BF16)

    def to_home(chunk):
        if chunk == 0:
            for stream in answer_flows:
                receive(stream, mid)
        else:
            receive(grads_flow, mid)
        one_hot = (gather_split, gather)[chunk]
        for i in range(4):
            home_out[chunk, i] = dot(one_hot[...], mid[i]).astype(BF16)
            place = out_ref.at[2 * chunk + i // 2, :, lanes(my_head, i)]

            @pl.loop(1, head_count)
            def _(step, i=i, place=place):
                other = head_peer(step)
                send(
                    home_out.at[chunk, i, stretch(other, rows)],
                    place,
                    out_send.at[chunk],
                    out_recv.at[chunk],
                    {"head": other},
                )

            place[...] = home_out[chunk, i, my_rows, :]

    from_heads(0)
    pl.semaphore_wait(plane_ready, plane - 1)
    pack_and_send(keys_flow, 0, 2)
    to_heads(1, range(2))
    pack_and_send(keys_flow, 2, PARTS)
    to_heads(1, range(2, 4))
    from_heads(1)
    pack_and_send(query_flows[0], 0, PARTS)
    keys_arrive()
    mean_line()
    pack_and_send(query_flows[1], 0, 2)
    mean_plane()
    pack_and_send(query_flows[1], 2, PARTS)
    mean_take()
    receive(query_flows[0], asked)
    attend(0)
    pack_and_send(answer_flows[0], 0, 2)
    receive(query_flows[1], asked)
    attend(1)
    grad_pack()
    pack_and_send(answer_flows[0], 2, PARTS, grad_to_plane)
    pack_and_send(answer_flows[1], 0, 2)
    grad_to_line()
    pack_and_send(answer_flows[1], 2, PARTS)
    grad_finish()
    pack_and_send(grads_flow, 0, 2)
    to_home(0)
    pack_and_send(grads_flow, 2, PARTS)
    to_home(1)

    for chunk in range(2):
        if head_count > 1:
            wait_bytes(home_out.at[chunk, :, others], out_recv.at[chunk])
            wait_bytes(home_out.at[chunk, :, others], out_send.at[chunk])
            wait_bytes(home.at[chunk, :, others], home_send.at[chunk])
    for stream in (keys_flow, *query_flows, *answer_flows, grads_flow):
        wait_sent(stream)
    wait_bytes(mean_line_bytes, line_send)
    wait_bytes(mean_plane_bytes, plane_send)
    wait_bytes(grad_plane_bytes, sum_plane_send)
    wait_bytes(grad_line_bytes, sum_line_send)


def per_device(queries, key_rows, value_rows, cotangent, cluster_of, order_tokens):
    seq_count = lax.axis_size("seq")
    head_count = lax.axis_size("head")
    plane = math.isqrt(seq_count)
    rows, full = queries.shape
    group_rows = cluster_of.shape[0]
    width = full // head_count
    half = width // 2
    combos = 4 * half // DH
    owned_count = group_rows // CLUSTER
    mean_slots = group_rows // seq_count
    capacity = mean_slots + mean_slots // 4
    slots = seq_count * capacity
    side = TILE * combos
    mean_rows = owned_count * combos
    mean_count = seq_count * owned_count
    mean_buf_rows = -(-seq_count * mean_rows // side) * side
    line_rows = seq_count // plane * mean_rows
    vmem = pltpu.VMEM
    scratch = [
        vmem((1, group_rows), jnp.int32),
        vmem((1, group_rows), jnp.int32),
        vmem((2, 4, group_rows, half), BF16),
        vmem((4, slots, half), BF16),
        vmem((2, slots * combos, DH), BF16),
        vmem((2, slots * combos, DH), BF16),
        vmem((4, group_rows, half), BF16),
        vmem((4, slots, half), BF16),
        vmem((mean_rows, DH), F32),
        vmem((mean_buf_rows, DH), BF16),
        vmem((combos, mean_buf_rows // combos, DH), BF16),
        vmem((4, slots, half), BF16),
        vmem((4, group_rows, half), BF16),
        vmem((4, group_rows, half), F32),
        vmem((combos, mean_count, DH), F32),
        vmem((seq_count * mean_rows, DH), F32),
        vmem((seq_count * mean_rows, DH), F32),
        vmem((line_rows, DH), F32),
        vmem((line_rows, DH), F32),
        vmem((mean_rows, DH), F32),
        vmem((2, slots * combos, DH), BF16),
        vmem((2, slots * combos, DH), BF16),
        vmem((2, 4, group_rows, half), BF16),
        vmem((slots, group_rows), BF16),
        vmem((group_rows, slots), BF16),
        vmem((slots, group_rows), BF16),
        vmem((group_rows, slots), BF16),
        vmem((slots, group_rows), BF16),
        vmem((group_rows, slots), BF16),
        vmem((side, side), BF16),
        vmem((side, side), BF16),
        vmem((group_rows, slots), F32),
    ]
    dma = pltpu.SemaphoreType.DMA
    by_chunk, by_flow, by_part = dma((2,)), dma((3,)), dma((3, PARTS))
    scratch += [by_chunk] * 3 + [by_flow, by_part] * 2 + [by_chunk] * 3 + [dma] * 8
    scratch += [pltpu.SemaphoreType.REGULAR]
    in_hbm = pl.BlockSpec(memory_space=pltpu.HBM)
    in_vmem = pl.BlockSpec(memory_space=pltpu.VMEM)
    staged = pl.pallas_call(
        functools.partial(kernel, seq_count, head_count, plane, capacity),
        out_shape=jax.ShapeDtypeStruct((4, rows, full), BF16),
        in_specs=[in_hbm] * 6,
        out_specs=in_vmem,
        scratch_shapes=scratch,
        compiler_params=pltpu.CompilerParams(
            collective_id=0, has_side_effects=True, vmem_limit_bytes=63 * 1024 * 1024
        ),
    )(
        queries,
        key_rows,
        value_rows,
        cotangent,
        cluster_of.reshape(1, group_rows),
        order_tokens.reshape(1, group_rows),
    )
    return tuple(staged[i] for i in range(4))


def solution(mesh):
    rows = P(("seq", "head"), None)
    return jax.shard_map(
        per_device,
        mesh=mesh,
        in_specs=(rows,) * 4 + (P("seq"),) * 2,
        out_specs=(rows,) * 4,
        check_vma=False,
    )
```

```python
import functools
import math

import jax
import jax.numpy as jnp
from jax import lax
from jax.experimental import pallas as pl
from jax.experimental.pallas import tpu as pltpu
from jax.sharding import PartitionSpec as P

DH = 128
CLUSTER = 256
MESH = pl.DeviceIdType.MESH
F32 = jnp.float32
BF16 = jnp.bfloat16

TILE = 32
PARTS = 4


def place_of(index, line, plane):
    at_line, at_plane = index // plane, index % plane
    pair = line // 2
    return (at_line % pair * 2 + at_line // pair) * plane + at_plane


def index_of(place, line, plane):
    at_line, at_plane = place // plane, place % plane
    return (at_line // 2 + at_line % 2 * (line // 2)) * plane + at_plane


def dot(a, b, dims=((1,), (0,))):
    return lax.dot_general(a, b, (dims, ((), ())), preferred_element_type=F32)


def as_column(row):
    return jnp.transpose(jnp.broadcast_to(row, (128, row.shape[1])))[:, :1]


def slot_vectors(group, rank_key, capacity, early, groups):
    group_col, key_col = as_column(group), as_column(rank_key)
    same = group_col == group
    rank_col = jnp.sum(jnp.where(same & (rank_key < key_col), 1.0, 0.0), axis=1, keepdims=True)
    rank_row = jnp.sum(jnp.where(same & (key_col < rank_key), 1.0, 0.0), axis=0, keepdims=True)

    def split(group, rank):
        late = early * groups + group * (capacity - early) + rank - early
        return jnp.where(rank < early, group * early + rank, late)

    return (
        group * capacity + rank_row,
        group_col * capacity + rank_col,
        split(group, rank_row),
        split(group_col, rank_col),
    )


def one_hot_rows(slot_row, count):
    slots = lax.broadcasted_iota(jnp.int32, (count, slot_row.shape[1]), 0).astype(F32)
    return jnp.where(slots == slot_row, 1.0, 0.0).astype(BF16)


def one_hot_columns(slot_col, count):
    slots = lax.broadcasted_iota(jnp.int32, (slot_col.shape[0], count), 1).astype(F32)
    return jnp.where(slots == slot_col, 1.0, 0.0).astype(BF16)


def kernel(
    seq_count, head_count, plane, capacity,
    q_ref, k_ref, v_ref, g_ref, cluster_ref, order_ref,
    out_ref,
    cluster_vec, order_vec, home, mid, send_buf, recv_buf, owned, asked, mean_msg, mean_buf, means,
    answers, results, inner, mean_acc, grad_msg, grad_plane, grad_part, grad_line, grad_sum,
    back_send, back_recv, home_out,
    spread, gather, spread_split, gather_split, unsort, resort, tile_perm, tile_back, hidden,
    home_own, home_send, home_recv, there_send, there_recv,
    back_send_sem, back_recv_sem, out_send, out_recv,
    table_sem, line_send, line_recv, plane_send, plane_recv,
    sum_plane_send, sum_plane_recv, sum_line_send, sum_line_recv, plane_ready,
):
    me = lax.axis_index("seq")
    my_head = lax.axis_index("head")
    rows, full = q_ref.shape
    width = full // head_count
    half = width // 2
    kinds = half // DH
    combos = 4 * kinds
    heads = width // DH
    group_rows = rows * head_count
    owned_count = group_rows // CLUSTER
    slots = seq_count * capacity
    early = capacity * 3 // 5
    part_peers = seq_count // PARTS
    side = TILE * combos
    mean_rows = owned_count * combos
    mean_count = seq_count * owned_count
    line = seq_count // plane
    my_line, my_plane = me // plane, lax.rem(me, plane)
    my_place = place_of(me, line, plane)
    my_part = my_place // part_peers
    scale = DH ** (-0.5)

    def head_peer(step):
        return lax.rem(my_head + step, head_count)

    def line_peer(step):
        return lax.rem(my_line + step, line)

    def plane_peer(step):
        return lax.rem(my_plane + step, plane)

    def stretch(index, size):
        return pl.ds(pl.multiple_of(index * size, size), size)

    def wait_bytes(ref, semaphore):
        pltpu.make_async_copy(ref, ref, semaphore).wait()

    def send(src, dst, send_sem, recv_sem, device):
        pltpu.make_async_remote_copy(
            src_ref=src,
            dst_ref=dst,
            send_sem=send_sem,
            recv_sem=recv_sem,
            device_id=device,
            device_id_type=MESH,
        ).start()

    barrier = pltpu.get_barrier_semaphore()

    def greet(semaphore, device):
        pl.semaphore_signal(semaphore, inc=1, device_id=device, device_id_type=MESH)

    @pl.loop(1, head_count)
    def _(step):
        greet(barrier, {"head": head_peer(step)})

    @pl.loop(1, line)
    def _(step):
        greet(barrier, {"seq": line_peer(step) * plane + my_plane})

    @pl.loop(1, plane)
    def _(step):
        greet(barrier, {"seq": my_line * plane + plane_peer(step)})

    table_copies = [
        pltpu.make_async_copy(cluster_ref, cluster_vec, table_sem.at[0]),
        pltpu.make_async_copy(order_ref, order_vec, table_sem.at[1]),
    ]
    for copy in table_copies:
        copy.start()

    pl.semaphore_wait(barrier, head_count - 1 + line - 1 + plane - 1)

    my_rows = stretch(my_head, rows)
    others = pl.ds(0, (head_count - 1) * rows)

    def lanes(head, i):
        return pl.ds(pl.multiple_of(head * width + (i % 2) * half, half), half)

    def to_heads(chunk, pairs=range(4)):
        for i in pairs:
            ref = ((k_ref, v_ref), (q_ref, g_ref))[chunk][i // 2]
            landing = home.at[chunk, i, my_rows]

            @pl.loop(1, head_count)
            def _(step, i=i, ref=ref, landing=landing):
                other = head_peer(step)
                send(
                    ref.at[:, lanes(other, i)],
                    landing,
                    home_send.at[chunk],
                    home_recv.at[chunk],
                    {"head": other},
                )

            pltpu.make_async_copy(
                ref.at[:, lanes(my_head, i)], landing, home_own.at[chunk]
            ).start()

    def from_heads(chunk):
        if head_count > 1:
            wait_bytes(home.at[chunk, :, others], home_recv.at[chunk])
        wait_bytes(home.at[chunk, :, pl.ds(0, rows)], home_own.at[chunk])

    to_heads(0)

    @pl.loop(1, plane)
    def _(step):
        greet(plane_ready, {"seq": my_line * plane + plane_peer(step)})

    for copy in table_copies:
        copy.wait()
    target = place_of(cluster_vec[...] // owned_count, line, plane).astype(F32)
    position = lax.broadcasted_iota(jnp.int32, (1, group_rows), 1).astype(F32)
    row, column, split_row, split_column = slot_vectors(
        target, position, capacity, early, seq_count
    )
    spread[...] = one_hot_rows(row, slots)
    gather[...] = one_hot_columns(column, slots)
    spread_split[...] = one_hot_rows(split_row, slots)
    gather_split[...] = one_hot_columns(split_column, slots)
    tokens_int = order_vec[...]
    tokens = tokens_int.astype(F32)
    source = place_of(tokens_int // group_rows, line, plane).astype(F32)
    row, column, _, split_column = slot_vectors(source, tokens, capacity, early, seq_count)
    unsort[...] = one_hot_rows(row, slots)
    resort[...] = one_hot_columns(column, slots)
    token_column = as_column(tokens)
    cell_column = (
        1 + lax.broadcasted_iota(jnp.int32, (group_rows, 1), 0) // CLUSTER
    ).astype(F32)
    slot_numbers = lax.broadcasted_iota(jnp.int32, (group_rows, slots), 1).astype(F32)
    held = slot_numbers == split_column
    slot_token = jnp.sum(jnp.where(held, token_column, 0.0), axis=0, keepdims=True)
    slot_cell = jnp.sum(jnp.where(held, cell_column, 0.0), axis=0, keepdims=True)
    hidden[...] = jnp.where(
        (cell_column == slot_cell) & (token_column <= slot_token), 0.0, -jnp.inf
    )
    first = lax.broadcasted_iota(jnp.int32, (side, side), 0)
    second = lax.broadcasted_iota(jnp.int32, (side, side), 1)
    tile_perm[...] = jnp.where(
        second == (first % combos) * TILE + first // combos, 1.0, 0.0
    ).astype(BF16)
    tile_back[...] = jnp.where(
        first == (second % combos) * TILE + second // combos, 1.0, 0.0
    ).astype(BF16)
    if mean_buf.shape[0] > seq_count * mean_rows:
        mean_buf[...] = jnp.zeros_like(mean_buf)

    def flow(size, base, one_hot, source_ref, out_buf, in_buf, send_sem, recv_sems):
        count = size * seq_count
        here = pl.ds(base * combos, count * combos)
        return (
            size, base, one_hot, source_ref, out_buf.at[here], in_buf.at[here], send_sem, recv_sems
        )

    def pack_part(stream, part):
        size, base, one_hot, source_ref, buf, _, _, _ = stream
        part_slots = size * part_peers
        start = pl.multiple_of(base + part * part_slots, TILE)
        if one_hot is None:
            pairs = [source_ref[i, pl.ds(start, part_slots), :] for i in range(4)]
        else:
            hot = one_hot[pl.ds(start, part_slots), :]
            pairs = [dot(hot, source_ref[i]).astype(BF16) for i in range(4)]
        groups = part_slots // TILE
        tiles = []
        for g in range(groups):
            pieces = []
            for pair in pairs:
                piece = pair[g * TILE : (g + 1) * TILE]
                pieces += [piece[:, lane : lane + DH] for lane in range(0, half, DH)]
            tiles.append(jnp.concatenate(pieces, axis=0))
        moved = dot(tile_perm[...], jnp.concatenate(tiles, axis=1)).astype(BF16)
        for g in range(groups):
            buf[pl.ds(pl.multiple_of(part * part_slots * combos + g * side, side), side), :] = (
                moved[:, g * DH : (g + 1) * DH]
            )

    def send_part(stream, part, extra):
        size, _, _, _, buf, dest, send_sem, recv_sems = stream
        block = size * combos
        mine = stretch(my_place, block)

        @pl.loop(0, part_peers)
        def _(step):
            place = part * part_peers + lax.rem(my_place + step * (plane + 1), part_peers)
            other = index_of(place, line, plane)

            @pl.when(place != my_place)
            def _():
                send(
                    buf.at[stretch(place, block)],
                    dest.at[mine],
                    send_sem,
                    recv_sems.at[my_part],
                    {"seq": other},
                )

            @pl.when(place == my_place)
            def _():
                dest[mine, :] = buf[mine, :]

            if extra is not None:
                extra(step)

    def pack_and_send(stream, first_step, last_step, extra=None):
        @pl.loop(first_step, last_step)
        def _(step):
            part = lax.rem(my_part + step, PARTS)
            pack_part(stream, part)
            also = None
            if extra is not None:
                also = lambda inner_step: extra((step - first_step) * part_peers + inner_step)
            send_part(stream, part, also)

    def receive(stream, target_ref):
        size, base, _, _, _, buf, _, recv_sems = stream
        block = size * combos
        part_slots = size * part_peers
        groups = part_slots // TILE
        whole = part_peers * block

        @pl.loop(0, PARTS)
        def _(step):
            part = lax.rem(my_part + PARTS - step, PARTS)

            @pl.when(part != my_part)
            def _():
                wait_bytes(buf.at[pl.ds(0, whole)], recv_sems.at[part])

            @pl.when(part == my_part)
            def _():
                wait_bytes(buf.at[pl.ds(0, whole - block)], recv_sems.at[part])

            tiles = [
                buf[pl.ds(pl.multiple_of(part * whole + g * side, side), side), :]
                for g in range(groups)
            ]
            moved = dot(tile_back[...], jnp.concatenate(tiles, axis=1)).astype(BF16)
            for g in range(groups):
                column = moved[:, g * DH : (g + 1) * DH]
                to = pl.ds(pl.multiple_of(base + part * part_slots + g * TILE, TILE), TILE)
                for i in range(4):
                    pieces = [
                        column[(i * kinds + j) * TILE : (i * kinds + j + 1) * TILE]
                        for j in range(kinds)
                    ]
                    target_ref[i, to, :] = jnp.concatenate(pieces, axis=1)

    def flows(chunk, one_hot, source_ref, split_hot, split_source, out_buf, in_buf, sends, recvs):
        first, second = out_buf.at[chunk], in_buf.at[chunk]
        late = early * seq_count
        if one_hot is not None:
            return flow(
                capacity, 0, one_hot, source_ref, first, second, sends.at[0], recvs.at[0]
            )
        return (
            flow(early, 0, split_hot, split_source, first, second, sends.at[1], recvs.at[1]),
            flow(
                capacity - early, late, split_hot, split_source, first, second,
                sends.at[2], recvs.at[2],
            ),
        )

    keys_flow = flows(
        0, spread, home.at[0], None, None, send_buf, recv_buf, there_send, there_recv
    )
    query_flows = flows(
        1, None, None, spread_split, home.at[1], send_buf, recv_buf, there_send, there_recv
    )
    answer_flows = flows(
        0, None, None, None, answers, back_send, back_recv, back_send_sem, back_recv_sem
    )
    grads_flow = flows(
        1, unsort, results, None, None, back_send, back_recv, back_send_sem, back_recv_sem
    )

    def wait_sent(stream):
        size, _, _, _, buf, _, send_sem, _ = stream
        wait_bytes(buf.at[pl.ds(0, (seq_count - 1) * size * combos)], send_sem)

    def keys_arrive():
        receive(keys_flow, mid)

        @pl.loop(0, 4)
        def _(i):
            owned[i] = dot(resort[...], mid[i]).astype(BF16)

    my_means = stretch(my_plane * line + my_line, mean_rows)

    def mean_line():
        for c in range(owned_count):
            for i in range(4):
                total = jnp.sum(
                    owned[i, c * CLUSTER : (c + 1) * CLUSTER, :].astype(F32),
                    axis=0,
                    keepdims=True,
                )
                for j in range(kinds):
                    at = c * combos + i * kinds + j
                    mean_msg[at : at + 1, :] = total[:, j * DH : (j + 1) * DH] / CLUSTER
        mean_buf[my_means, :] = mean_msg[...].astype(BF16)

        @pl.loop(1, line)
        def _(step):
            send(
                mean_buf.at[my_means],
                mean_buf.at[my_means],
                line_send,
                line_recv,
                {"seq": line_peer(step) * plane + my_plane},
            )

    mean_line_bytes = mean_buf.at[pl.ds(0, (line - 1) * mean_rows)]
    mean_plane_bytes = mean_buf.at[pl.ds(0, (plane - 1) * line * mean_rows)]

    def mean_plane():
        wait_bytes(mean_line_bytes, line_recv)
        my_lines = stretch(my_plane, line * mean_rows)

        @pl.loop(1, plane)
        def _(step):
            send(
                mean_buf.at[my_lines],
                mean_buf.at[my_lines],
                plane_send,
                plane_recv,
                {"seq": my_line * plane + plane_peer(step)},
            )

    def mean_take():
        wait_bytes(mean_plane_bytes, plane_recv)
        for g in range(mean_buf.shape[0] // side):
            moved = dot(tile_back[...], mean_buf[g * side : (g + 1) * side, :]).astype(BF16)
            for i in range(combos):
                means[i, g * TILE : (g + 1) * TILE, :] = moved[i * TILE : (i + 1) * TILE, :]

    def attend(which):
        size, base = query_flows[which][:2]
        part = pl.ds(base, size * seq_count)

        @pl.loop(0, heads)
        def _(h):
            pair = h // kinds
            lane = pl.ds(pl.multiple_of(lax.rem(h, kinds) * DH, DH), DH)
            keys = jnp.concatenate([owned[pair, :, lane], means[h, :mean_count, :]], axis=0)
            values = jnp.concatenate(
                [owned[2 + pair, :, lane], means[heads + h, :mean_count, :]], axis=0
            )
            queries = asked[pair, part, lane]
            grads = asked[2 + pair, part, lane]
            scores = dot(keys, queries, ((1,), (1,))) * scale
            scores = jnp.concatenate(
                [scores[:group_rows] + hidden[:, part], scores[group_rows:]], axis=0
            )
            top = jnp.max(scores, axis=0, keepdims=True)
            powers = jnp.exp(scores - top)
            weights = powers * (1.0 / jnp.sum(powers, axis=0, keepdims=True))
            rounded = weights.astype(BF16)
            weight_grads = dot(values, grads, ((1,), (1,)))
            delta = jnp.sum(weights * weight_grads, axis=0, keepdims=True)
            steps = (weights * (weight_grads - delta)).astype(BF16)
            answers[pair, part, lane] = dot(rounded, values, ((0,), (0,))).astype(BF16)
            answers[2 + pair, part, lane] = (scale * dot(steps, keys, ((0,), (0,)))).astype(BF16)
            key_grads = scale * dot(steps, queries)
            value_grads = dot(rounded, grads)
            if which == 0:
                inner[pair, :, lane] = key_grads[:group_rows]
                inner[2 + pair, :, lane] = value_grads[:group_rows]
                mean_acc[h] = key_grads[group_rows:]
                mean_acc[heads + h] = value_grads[group_rows:]
            else:
                inner[pair, :, lane] += key_grads[:group_rows]
                inner[2 + pair, :, lane] += value_grads[:group_rows]
                mean_acc[h] += key_grads[group_rows:]
                mean_acc[heads + h] += value_grads[group_rows:]

    plane_size = line * mean_rows

    def grad_pack():
        for i in range(combos):
            grad_msg[pl.ds(i, mean_count, stride=combos), :] = mean_acc[i]
        mine = stretch(my_plane, plane_size)
        grad_plane[mine, :] = grad_msg[mine, :]

    pieces = (plane - 1) * line
    piece_steps = 2 * part_peers
    pieces_per_step = -(-pieces // piece_steps)

    def grad_to_plane(step):
        for i in range(pieces_per_step):
            number = step * pieces_per_step + i

            @pl.when(number < pieces)
            def _(number=number):
                other = plane_peer(number // line + 1)
                at_line = number % line
                send(
                    grad_msg.at[stretch(other * line + at_line, mean_rows)],
                    grad_plane.at[stretch(my_plane * line + at_line, mean_rows)],
                    sum_plane_send,
                    sum_plane_recv,
                    {"seq": my_line * plane + other},
                )

    grad_plane_bytes = grad_plane.at[pl.ds(0, (plane - 1) * plane_size)]
    grad_line_bytes = grad_line.at[pl.ds(0, (line - 1) * mean_rows)]

    def grad_to_line():
        wait_bytes(grad_plane_bytes, sum_plane_recv)
        total = grad_plane[:plane_size, :]
        for i in range(1, plane):
            total = total + grad_plane[i * plane_size : (i + 1) * plane_size, :]
        grad_part[...] = total
        mine = stretch(my_line, mean_rows)

        @pl.loop(1, line)
        def _(step):
            other = line_peer(step)
            send(
                grad_part.at[stretch(other, mean_rows)],
                grad_line.at[mine],
                sum_line_send,
                sum_line_recv,
                {"seq": other * plane + my_plane},
            )

        grad_line[mine, :] = grad_part[mine, :]

    def grad_finish():
        wait_bytes(grad_line_bytes, sum_line_recv)
        total = grad_line[:mean_rows, :]
        for i in range(1, line):
            total = total + grad_line[i * mean_rows : (i + 1) * mean_rows, :]
        grad_sum[...] = total / CLUSTER
        for i in range(4):
            for c in range(owned_count):
                part = slice(c * CLUSTER, (c + 1) * CLUSTER)
                for j in range(kinds):
                    lane = slice(j * DH, (j + 1) * DH)
                    at = c * combos + i * kinds + j
                    results[i, part, lane] = (
                        inner[i, part, lane] + grad_sum[at : at + 1, :]
                    ).astype(BF16)

    def to_home(chunk):
        if chunk == 0:
            for stream in answer_flows:
                receive(stream, mid)
        else:
            receive(grads_flow, mid)
        one_hot = (gather_split, gather)[chunk]
        for i in range(4):
            home_out[chunk, i] = dot(one_hot[...], mid[i]).astype(BF16)
            place = out_ref.at[2 * chunk + i // 2, :, lanes(my_head, i)]

            @pl.loop(1, head_count)
            def _(step, i=i, place=place):
                other = head_peer(step)
                send(
                    home_out.at[chunk, i, stretch(other, rows)],
                    place,
                    out_send.at[chunk],
                    out_recv.at[chunk],
                    {"head": other},
                )

            place[...] = home_out[chunk, i, my_rows, :]

    from_heads(0)
    pl.semaphore_wait(plane_ready, plane - 1)
    pack_and_send(keys_flow, 0, 2)
    to_heads(1, range(2))
    pack_and_send(keys_flow, 2, PARTS)
    to_heads(1, range(2, 4))
    from_heads(1)
    pack_and_send(query_flows[0], 0, 3)
    keys_arrive()
    mean_line()
    pack_and_send(query_flows[0], 3, PARTS)
    pack_and_send(query_flows[1], 0, 1)
    mean_plane()
    pack_and_send(query_flows[1], 1, PARTS)
    mean_take()
    receive(query_flows[0], asked)
    attend(0)
    pack_and_send(answer_flows[0], 0, 2)
    receive(query_flows[1], asked)
    attend(1)
    grad_pack()
    pack_and_send(answer_flows[0], 2, PARTS, grad_to_plane)
    pack_and_send(answer_flows[1], 0, 2)
    grad_to_line()
    pack_and_send(answer_flows[1], 2, PARTS)
    grad_finish()
    pack_and_send(grads_flow, 0, 2)
    to_home(0)
    pack_and_send(grads_flow, 2, PARTS)
    to_home(1)

    for chunk in range(2):
        if head_count > 1:
            wait_bytes(home_out.at[chunk, :, others], out_recv.at[chunk])
            wait_bytes(home_out.at[chunk, :, others], out_send.at[chunk])
            wait_bytes(home.at[chunk, :, others], home_send.at[chunk])
    for stream in (keys_flow, *query_flows, *answer_flows, grads_flow):
        wait_sent(stream)
    wait_bytes(mean_line_bytes, line_send)
    wait_bytes(mean_plane_bytes, plane_send)
    wait_bytes(grad_plane_bytes, sum_plane_send)
    wait_bytes(grad_line_bytes, sum_line_send)


def per_device(queries, key_rows, value_rows, cotangent, cluster_of, order_tokens):
    seq_count = lax.axis_size("seq")
    head_count = lax.axis_size("head")
    plane = math.isqrt(seq_count)
    rows, full = queries.shape
    group_rows = cluster_of.shape[0]
    width = full // head_count
    half = width // 2
    combos = 4 * half // DH
    owned_count = group_rows // CLUSTER
    mean_slots = group_rows // seq_count
    capacity = mean_slots + mean_slots // 4
    slots = seq_count * capacity
    side = TILE * combos
    mean_rows = owned_count * combos
    mean_count = seq_count * owned_count
    mean_buf_rows = -(-seq_count * mean_rows // side) * side
    line_rows = seq_count // plane * mean_rows
    vmem = pltpu.VMEM
    scratch = [
        vmem((1, group_rows), jnp.int32),
        vmem((1, group_rows), jnp.int32),
        vmem((2, 4, group_rows, half), BF16),
        vmem((4, slots, half), BF16),
        vmem((2, slots * combos, DH), BF16),
        vmem((2, slots * combos, DH), BF16),
        vmem((4, group_rows, half), BF16),
        vmem((4, slots, half), BF16),
        vmem((mean_rows, DH), F32),
        vmem((mean_buf_rows, DH), BF16),
        vmem((combos, mean_buf_rows // combos, DH), BF16),
        vmem((4, slots, half), BF16),
        vmem((4, group_rows, half), BF16),
        vmem((4, group_rows, half), F32),
        vmem((combos, mean_count, DH), F32),
        vmem((seq_count * mean_rows, DH), F32),
        vmem((seq_count * mean_rows, DH), F32),
        vmem((line_rows, DH), F32),
        vmem((line_rows, DH), F32),
        vmem((mean_rows, DH), F32),
        vmem((2, slots * combos, DH), BF16),
        vmem((2, slots * combos, DH), BF16),
        vmem((2, 4, group_rows, half), BF16),
        vmem((slots, group_rows), BF16),
        vmem((group_rows, slots), BF16),
        vmem((slots, group_rows), BF16),
        vmem((group_rows, slots), BF16),
        vmem((slots, group_rows), BF16),
        vmem((group_rows, slots), BF16),
        vmem((side, side), BF16),
        vmem((side, side), BF16),
        vmem((group_rows, slots), F32),
    ]
    dma = pltpu.SemaphoreType.DMA
    by_chunk, by_flow, by_part = dma((2,)), dma((3,)), dma((3, PARTS))
    scratch += [by_chunk] * 3 + [by_flow, by_part] * 2 + [by_chunk] * 3 + [dma] * 8
    scratch += [pltpu.SemaphoreType.REGULAR]
    in_hbm = pl.BlockSpec(memory_space=pltpu.HBM)
    in_vmem = pl.BlockSpec(memory_space=pltpu.VMEM)
    staged = pl.pallas_call(
        functools.partial(kernel, seq_count, head_count, plane, capacity),
        out_shape=jax.ShapeDtypeStruct((4, rows, full), BF16),
        in_specs=[in_hbm] * 6,
        out_specs=in_vmem,
        scratch_shapes=scratch,
        compiler_params=pltpu.CompilerParams(
            collective_id=0, has_side_effects=True, vmem_limit_bytes=63 * 1024 * 1024
        ),
    )(
        queries,
        key_rows,
        value_rows,
        cotangent,
        cluster_of.reshape(1, group_rows),
        order_tokens.reshape(1, group_rows),
    )
    return tuple(staged[i] for i in range(4))


def solution(mesh):
    rows = P(("seq", "head"), None)
    return jax.shard_map(
        per_device,
        mesh=mesh,
        in_specs=(rows,) * 4 + (P("seq"),) * 2,
        out_specs=(rows,) * 4,
        check_vma=False,
    )
```

```python
import functools
import math

import jax
import jax.numpy as jnp
from jax import lax
from jax.experimental import pallas as pl
from jax.experimental.pallas import tpu as pltpu
from jax.sharding import PartitionSpec as P

DH = 128
CLUSTER = 256
MESH = pl.DeviceIdType.MESH
F32 = jnp.float32
BF16 = jnp.bfloat16

TILE = 32
PARTS = 4


def place_of(index, line, plane):
    at_line, at_plane = index // plane, index % plane
    pair = line // 2
    return (at_line % pair * 2 + at_line // pair) * plane + at_plane


def index_of(place, line, plane):
    at_line, at_plane = place // plane, place % plane
    return (at_line // 2 + at_line % 2 * (line // 2)) * plane + at_plane


def dot(a, b, dims=((1,), (0,))):
    return lax.dot_general(a, b, (dims, ((), ())), preferred_element_type=F32)


def as_column(row):
    return jnp.transpose(jnp.broadcast_to(row, (128, row.shape[1])))[:, :1]


def slot_vectors(group, rank_key, capacity, early, groups):
    group_col, key_col = as_column(group), as_column(rank_key)
    same = group_col == group
    rank_col = jnp.sum(jnp.where(same & (rank_key < key_col), 1.0, 0.0), axis=1, keepdims=True)
    rank_row = jnp.sum(jnp.where(same & (key_col < rank_key), 1.0, 0.0), axis=0, keepdims=True)

    def split(group, rank):
        late = early * groups + group * (capacity - early) + rank - early
        return jnp.where(rank < early, group * early + rank, late)

    return (
        group * capacity + rank_row,
        group_col * capacity + rank_col,
        split(group, rank_row),
        split(group_col, rank_col),
    )


def one_hot_rows(slot_row, count):
    slots = lax.broadcasted_iota(jnp.int32, (count, slot_row.shape[1]), 0).astype(F32)
    return jnp.where(slots == slot_row, 1.0, 0.0).astype(BF16)


def one_hot_columns(slot_col, count):
    slots = lax.broadcasted_iota(jnp.int32, (slot_col.shape[0], count), 1).astype(F32)
    return jnp.where(slots == slot_col, 1.0, 0.0).astype(BF16)


def kernel(
    seq_count, head_count, plane, capacity,
    q_ref, k_ref, v_ref, g_ref, cluster_ref, order_ref,
    out_ref,
    cluster_vec, order_vec, home, mid, send_buf, recv_buf, owned, asked, mean_msg, mean_buf, means,
    answers, results, inner, mean_acc, grad_msg, grad_plane, grad_part, grad_line, grad_sum,
    back_send, back_recv, home_out,
    spread, gather, spread_split, gather_split, unsort, resort, tile_perm, tile_back, hidden,
    home_own, home_send, home_recv, there_send, there_recv,
    back_send_sem, back_recv_sem, out_send, out_recv,
    table_sem, line_send, line_recv, plane_send, plane_recv,
    sum_plane_send, sum_plane_recv, sum_line_send, sum_line_recv, plane_ready,
):
    me = lax.axis_index("seq")
    my_head = lax.axis_index("head")
    rows, full = q_ref.shape
    width = full // head_count
    half = width // 2
    kinds = half // DH
    combos = 4 * kinds
    heads = width // DH
    group_rows = rows * head_count
    owned_count = group_rows // CLUSTER
    slots = seq_count * capacity
    early = capacity * 3 // 5
    part_peers = seq_count // PARTS
    side = TILE * combos
    mean_rows = owned_count * combos
    mean_count = seq_count * owned_count
    line = seq_count // plane
    my_line, my_plane = me // plane, lax.rem(me, plane)
    my_place = place_of(me, line, plane)
    my_part = my_place // part_peers
    scale = DH ** (-0.5)

    def head_peer(step):
        return lax.rem(my_head + step, head_count)

    def line_peer(step):
        return lax.rem(my_line + step, line)

    def plane_peer(step):
        return lax.rem(my_plane + step, plane)

    def stretch(index, size):
        return pl.ds(pl.multiple_of(index * size, size), size)

    def wait_bytes(ref, semaphore):
        pltpu.make_async_copy(ref, ref, semaphore).wait()

    def send(src, dst, send_sem, recv_sem, device):
        pltpu.make_async_remote_copy(
            src_ref=src,
            dst_ref=dst,
            send_sem=send_sem,
            recv_sem=recv_sem,
            device_id=device,
            device_id_type=MESH,
        ).start()

    barrier = pltpu.get_barrier_semaphore()

    def greet(semaphore, device):
        pl.semaphore_signal(semaphore, inc=1, device_id=device, device_id_type=MESH)

    @pl.loop(1, head_count)
    def _(step):
        greet(barrier, {"head": head_peer(step)})

    @pl.loop(1, line)
    def _(step):
        greet(barrier, {"seq": line_peer(step) * plane + my_plane})

    @pl.loop(1, plane)
    def _(step):
        greet(barrier, {"seq": my_line * plane + plane_peer(step)})

    table_copies = [
        pltpu.make_async_copy(cluster_ref, cluster_vec, table_sem.at[0]),
        pltpu.make_async_copy(order_ref, order_vec, table_sem.at[1]),
    ]
    for copy in table_copies:
        copy.start()

    pl.semaphore_wait(barrier, head_count - 1 + line - 1 + plane - 1)

    my_rows = stretch(my_head, rows)
    others = pl.ds(0, (head_count - 1) * rows)

    def lanes(head, i):
        return pl.ds(pl.multiple_of(head * width + (i % 2) * half, half), half)

    def to_heads(chunk, pairs=range(4)):
        for i in pairs:
            ref = ((k_ref, v_ref), (q_ref, g_ref))[chunk][i // 2]
            landing = home.at[chunk, i, my_rows]

            @pl.loop(1, head_count)
            def _(step, i=i, ref=ref, landing=landing):
                other = head_peer(step)
                send(
                    ref.at[:, lanes(other, i)],
                    landing,
                    home_send.at[chunk],
                    home_recv.at[chunk],
                    {"head": other},
                )

            pltpu.make_async_copy(
                ref.at[:, lanes(my_head, i)], landing, home_own.at[chunk]
            ).start()

    def from_heads(chunk):
        if head_count > 1:
            wait_bytes(home.at[chunk, :, others], home_recv.at[chunk])
        wait_bytes(home.at[chunk, :, pl.ds(0, rows)], home_own.at[chunk])

    to_heads(0)

    @pl.loop(1, plane)
    def _(step):
        greet(plane_ready, {"seq": my_line * plane + plane_peer(step)})

    for copy in table_copies:
        copy.wait()
    target = place_of(cluster_vec[...] // owned_count, line, plane).astype(F32)
    position = lax.broadcasted_iota(jnp.int32, (1, group_rows), 1).astype(F32)
    row, column, split_row, split_column = slot_vectors(
        target, position, capacity, early, seq_count
    )
    spread[...] = one_hot_rows(row, slots)
    gather[...] = one_hot_columns(column, slots)
    spread_split[...] = one_hot_rows(split_row, slots)
    gather_split[...] = one_hot_columns(split_column, slots)
    tokens_int = order_vec[...]
    tokens = tokens_int.astype(F32)
    source = place_of(tokens_int // group_rows, line, plane).astype(F32)
    row, column, _, split_column = slot_vectors(source, tokens, capacity, early, seq_count)
    unsort[...] = one_hot_rows(row, slots)
    resort[...] = one_hot_columns(column, slots)
    token_column = as_column(tokens)
    cell_column = (
        1 + lax.broadcasted_iota(jnp.int32, (group_rows, 1), 0) // CLUSTER
    ).astype(F32)
    slot_numbers = lax.broadcasted_iota(jnp.int32, (group_rows, slots), 1).astype(F32)
    held = slot_numbers == split_column
    slot_token = jnp.sum(jnp.where(held, token_column, 0.0), axis=0, keepdims=True)
    slot_cell = jnp.sum(jnp.where(held, cell_column, 0.0), axis=0, keepdims=True)
    hidden[...] = jnp.where(
        (cell_column == slot_cell) & (token_column <= slot_token), 0.0, -jnp.inf
    )
    first = lax.broadcasted_iota(jnp.int32, (side, side), 0)
    second = lax.broadcasted_iota(jnp.int32, (side, side), 1)
    tile_perm[...] = jnp.where(
        second == (first % combos) * TILE + first // combos, 1.0, 0.0
    ).astype(BF16)
    tile_back[...] = jnp.where(
        first == (second % combos) * TILE + second // combos, 1.0, 0.0
    ).astype(BF16)
    if mean_buf.shape[0] > seq_count * mean_rows:
        mean_buf[...] = jnp.zeros_like(mean_buf)

    def flow(size, base, one_hot, source_ref, out_buf, in_buf, send_sem, recv_sems):
        count = size * seq_count
        here = pl.ds(base * combos, count * combos)
        return (
            size, base, one_hot, source_ref, out_buf.at[here], in_buf.at[here], send_sem, recv_sems
        )

    def pack_part(stream, part):
        size, base, one_hot, source_ref, buf, _, _, _ = stream
        part_slots = size * part_peers
        start = pl.multiple_of(base + part * part_slots, TILE)
        if one_hot is None:
            pairs = [source_ref[i, pl.ds(start, part_slots), :] for i in range(4)]
        else:
            hot = one_hot[pl.ds(start, part_slots), :]
            pairs = [dot(hot, source_ref[i]).astype(BF16) for i in range(4)]
        groups = part_slots // TILE
        tiles = []
        for g in range(groups):
            pieces = []
            for pair in pairs:
                piece = pair[g * TILE : (g + 1) * TILE]
                pieces += [piece[:, lane : lane + DH] for lane in range(0, half, DH)]
            tiles.append(jnp.concatenate(pieces, axis=0))
        moved = dot(tile_perm[...], jnp.concatenate(tiles, axis=1)).astype(BF16)
        for g in range(groups):
            buf[pl.ds(pl.multiple_of(part * part_slots * combos + g * side, side), side), :] = (
                moved[:, g * DH : (g + 1) * DH]
            )

    def send_part(stream, part, extra):
        size, _, _, _, buf, dest, send_sem, recv_sems = stream
        block = size * combos
        mine = stretch(my_place, block)

        @pl.loop(0, part_peers)
        def _(step):
            place = part * part_peers + lax.rem(my_place + step * (plane + 1), part_peers)
            other = index_of(place, line, plane)

            @pl.when(place != my_place)
            def _():
                send(
                    buf.at[stretch(place, block)],
                    dest.at[mine],
                    send_sem,
                    recv_sems.at[my_part],
                    {"seq": other},
                )

            @pl.when(place == my_place)
            def _():
                dest[mine, :] = buf[mine, :]

            if extra is not None:
                extra(step)

    def pack_and_send(stream, first_step, last_step, extra=None):
        @pl.loop(first_step, last_step)
        def _(step):
            part = lax.rem(my_part + step, PARTS)
            pack_part(stream, part)
            also = None
            if extra is not None:
                also = lambda inner_step: extra((step - first_step) * part_peers + inner_step)
            send_part(stream, part, also)

    def receive(stream, target_ref):
        size, base, _, _, _, buf, _, recv_sems = stream
        block = size * combos
        part_slots = size * part_peers
        groups = part_slots // TILE
        whole = part_peers * block

        @pl.loop(0, PARTS)
        def _(step):
            part = lax.rem(my_part + PARTS - step, PARTS)

            @pl.when(part != my_part)
            def _():
                wait_bytes(buf.at[pl.ds(0, whole)], recv_sems.at[part])

            @pl.when(part == my_part)
            def _():
                wait_bytes(buf.at[pl.ds(0, whole - block)], recv_sems.at[part])

            tiles = [
                buf[pl.ds(pl.multiple_of(part * whole + g * side, side), side), :]
                for g in range(groups)
            ]
            moved = dot(tile_back[...], jnp.concatenate(tiles, axis=1)).astype(BF16)
            for g in range(groups):
                column = moved[:, g * DH : (g + 1) * DH]
                to = pl.ds(pl.multiple_of(base + part * part_slots + g * TILE, TILE), TILE)
                for i in range(4):
                    pieces = [
                        column[(i * kinds + j) * TILE : (i * kinds + j + 1) * TILE]
                        for j in range(kinds)
                    ]
                    target_ref[i, to, :] = jnp.concatenate(pieces, axis=1)

    def flows(chunk, one_hot, source_ref, split_hot, split_source, out_buf, in_buf, sends, recvs):
        first, second = out_buf.at[chunk], in_buf.at[chunk]
        late = early * seq_count
        if one_hot is not None:
            return flow(
                capacity, 0, one_hot, source_ref, first, second, sends.at[0], recvs.at[0]
            )
        return (
            flow(early, 0, split_hot, split_source, first, second, sends.at[1], recvs.at[1]),
            flow(
                capacity - early, late, split_hot, split_source, first, second,
                sends.at[2], recvs.at[2],
            ),
        )

    keys_flow = flows(
        0, spread, home.at[0], None, None, send_buf, recv_buf, there_send, there_recv
    )
    query_flows = flows(
        1, None, None, spread_split, home.at[1], send_buf, recv_buf, there_send, there_recv
    )
    answer_flows = flows(
        0, None, None, None, answers, back_send, back_recv, back_send_sem, back_recv_sem
    )
    grads_flow = flows(
        1, unsort, results, None, None, back_send, back_recv, back_send_sem, back_recv_sem
    )

    def wait_sent(stream):
        size, _, _, _, buf, _, send_sem, _ = stream
        wait_bytes(buf.at[pl.ds(0, (seq_count - 1) * size * combos)], send_sem)

    def keys_arrive():
        receive(keys_flow, mid)

        @pl.loop(0, 4)
        def _(i):
            owned[i] = dot(resort[...], mid[i]).astype(BF16)

    my_means = stretch(my_plane * line + my_line, mean_rows)

    def mean_line():
        for c in range(owned_count):
            for i in range(4):
                total = jnp.sum(
                    owned[i, c * CLUSTER : (c + 1) * CLUSTER, :].astype(F32),
                    axis=0,
                    keepdims=True,
                )
                for j in range(kinds):
                    at = c * combos + i * kinds + j
                    mean_msg[at : at + 1, :] = total[:, j * DH : (j + 1) * DH] / CLUSTER
        mean_buf[my_means, :] = mean_msg[...].astype(BF16)

        @pl.loop(1, line)
        def _(step):
            send(
                mean_buf.at[my_means],
                mean_buf.at[my_means],
                line_send,
                line_recv,
                {"seq": line_peer(step) * plane + my_plane},
            )

    mean_line_bytes = mean_buf.at[pl.ds(0, (line - 1) * mean_rows)]
    mean_plane_bytes = mean_buf.at[pl.ds(0, (plane - 1) * line * mean_rows)]

    def mean_plane():
        wait_bytes(mean_line_bytes, line_recv)
        my_lines = stretch(my_plane, line * mean_rows)

        @pl.loop(1, plane)
        def _(step):
            send(
                mean_buf.at[my_lines],
                mean_buf.at[my_lines],
                plane_send,
                plane_recv,
                {"seq": my_line * plane + plane_peer(step)},
            )

    def mean_take():
        wait_bytes(mean_plane_bytes, plane_recv)
        for g in range(mean_buf.shape[0] // side):
            moved = dot(tile_back[...], mean_buf[g * side : (g + 1) * side, :]).astype(BF16)
            for i in range(combos):
                means[i, g * TILE : (g + 1) * TILE, :] = moved[i * TILE : (i + 1) * TILE, :]

    def attend(which):
        size, base = query_flows[which][:2]
        part = pl.ds(base, size * seq_count)

        @pl.loop(0, heads)
        def _(h):
            pair = h // kinds
            lane = pl.ds(pl.multiple_of(lax.rem(h, kinds) * DH, DH), DH)
            keys = jnp.concatenate([owned[pair, :, lane], means[h, :mean_count, :]], axis=0)
            values = jnp.concatenate(
                [owned[2 + pair, :, lane], means[heads + h, :mean_count, :]], axis=0
            )
            queries = asked[pair, part, lane]
            grads = asked[2 + pair, part, lane]
            scores = dot(keys, queries, ((1,), (1,))) * scale
            scores = jnp.concatenate(
                [scores[:group_rows] + hidden[:, part], scores[group_rows:]], axis=0
            )
            top = jnp.max(scores, axis=0, keepdims=True)
            powers = jnp.exp(scores - top)
            weights = powers * (1.0 / jnp.sum(powers, axis=0, keepdims=True))
            rounded = weights.astype(BF16)
            weight_grads = dot(values, grads, ((1,), (1,)))
            delta = jnp.sum(weights * weight_grads, axis=0, keepdims=True)
            steps = (weights * (weight_grads - delta)).astype(BF16)
            answers[pair, part, lane] = dot(rounded, values, ((0,), (0,))).astype(BF16)
            answers[2 + pair, part, lane] = (scale * dot(steps, keys, ((0,), (0,)))).astype(BF16)
            key_grads = scale * dot(steps, queries)
            value_grads = dot(rounded, grads)
            if which == 0:
                inner[pair, :, lane] = key_grads[:group_rows]
                inner[2 + pair, :, lane] = value_grads[:group_rows]
                mean_acc[h] = key_grads[group_rows:]
                mean_acc[heads + h] = value_grads[group_rows:]
            else:
                inner[pair, :, lane] += key_grads[:group_rows]
                inner[2 + pair, :, lane] += value_grads[:group_rows]
                mean_acc[h] += key_grads[group_rows:]
                mean_acc[heads + h] += value_grads[group_rows:]

    plane_size = line * mean_rows

    def grad_pack():
        for i in range(combos):
            grad_msg[pl.ds(i, mean_count, stride=combos), :] = mean_acc[i]
        mine = stretch(my_plane, plane_size)
        grad_plane[mine, :] = grad_msg[mine, :]

    pieces = (plane - 1) * line
    piece_steps = 2 * part_peers
    pieces_per_step = -(-pieces // piece_steps)

    def grad_to_plane(step):
        for i in range(pieces_per_step):
            number = step * pieces_per_step + i

            @pl.when(number < pieces)
            def _(number=number):
                other = plane_peer(number // line + 1)
                at_line = number % line
                send(
                    grad_msg.at[stretch(other * line + at_line, mean_rows)],
                    grad_plane.at[stretch(my_plane * line + at_line, mean_rows)],
                    sum_plane_send,
                    sum_plane_recv,
                    {"seq": my_line * plane + other},
                )

    grad_plane_bytes = grad_plane.at[pl.ds(0, (plane - 1) * plane_size)]
    grad_line_bytes = grad_line.at[pl.ds(0, (line - 1) * mean_rows)]

    def grad_to_line():
        wait_bytes(grad_plane_bytes, sum_plane_recv)
        total = grad_plane[:plane_size, :]
        for i in range(1, plane):
            total = total + grad_plane[i * plane_size : (i + 1) * plane_size, :]
        grad_part[...] = total
        mine = stretch(my_line, mean_rows)

        @pl.loop(1, line)
        def _(step):
            other = line_peer(step)
            send(
                grad_part.at[stretch(other, mean_rows)],
                grad_line.at[mine],
                sum_line_send,
                sum_line_recv,
                {"seq": other * plane + my_plane},
            )

        grad_line[mine, :] = grad_part[mine, :]

    def grad_finish():
        wait_bytes(grad_line_bytes, sum_line_recv)
        total = grad_line[:mean_rows, :]
        for i in range(1, line):
            total = total + grad_line[i * mean_rows : (i + 1) * mean_rows, :]
        grad_sum[...] = total / CLUSTER
        for i in range(4):
            for c in range(owned_count):
                part = slice(c * CLUSTER, (c + 1) * CLUSTER)
                for j in range(kinds):
                    lane = slice(j * DH, (j + 1) * DH)
                    at = c * combos + i * kinds + j
                    results[i, part, lane] = (
                        inner[i, part, lane] + grad_sum[at : at + 1, :]
                    ).astype(BF16)

    def to_home(chunk):
        if chunk == 0:
            for stream in answer_flows:
                receive(stream, mid)
        else:
            receive(grads_flow, mid)
        one_hot = (gather_split, gather)[chunk]
        for i in range(4):
            home_out[chunk, i] = dot(one_hot[...], mid[i]).astype(BF16)
            place = out_ref.at[2 * chunk + i // 2, :, lanes(my_head, i)]

            @pl.loop(1, head_count)
            def _(step, i=i, place=place):
                other = head_peer(step)
                send(
                    home_out.at[chunk, i, stretch(other, rows)],
                    place,
                    out_send.at[chunk],
                    out_recv.at[chunk],
                    {"head": other},
                )

            pltpu.make_async_copy(
                home_out.at[chunk, i, my_rows], place, home_own.at[chunk]
            ).start()

    from_heads(0)
    pl.semaphore_wait(plane_ready, plane - 1)
    pack_and_send(keys_flow, 0, 2)
    to_heads(1, range(2))
    pack_and_send(keys_flow, 2, PARTS)
    to_heads(1, range(2, 4))
    from_heads(1)
    pack_and_send(query_flows[0], 0, 3)
    keys_arrive()
    mean_line()
    pack_and_send(query_flows[0], 3, PARTS)
    pack_and_send(query_flows[1], 0, 1)
    mean_plane()
    pack_and_send(query_flows[1], 1, PARTS)
    mean_take()
    receive(query_flows[0], asked)
    attend(0)
    pack_and_send(answer_flows[0], 0, 2)
    receive(query_flows[1], asked)
    attend(1)
    grad_pack()
    pack_and_send(answer_flows[0], 2, PARTS, grad_to_plane)
    pack_and_send(answer_flows[1], 0, 2)
    grad_to_line()
    pack_and_send(answer_flows[1], 2, PARTS)
    grad_finish()
    pack_and_send(grads_flow, 0, 2)
    to_home(0)
    pack_and_send(grads_flow, 2, PARTS)
    to_home(1)

    for chunk in range(2):
        if head_count > 1:
            wait_bytes(home_out.at[chunk, :, others], out_recv.at[chunk])
            wait_bytes(home_out.at[chunk, :, others], out_send.at[chunk])
            wait_bytes(home.at[chunk, :, others], home_send.at[chunk])
    for chunk in range(2):
        wait_bytes(home_out.at[chunk, :, pl.ds(0, rows)], home_own.at[chunk])
    for stream in (keys_flow, *query_flows, *answer_flows, grads_flow):
        wait_sent(stream)
    wait_bytes(mean_line_bytes, line_send)
    wait_bytes(mean_plane_bytes, plane_send)
    wait_bytes(grad_plane_bytes, sum_plane_send)
    wait_bytes(grad_line_bytes, sum_line_send)


def per_device(queries, key_rows, value_rows, cotangent, cluster_of, order_tokens):
    seq_count = lax.axis_size("seq")
    head_count = lax.axis_size("head")
    plane = math.isqrt(seq_count)
    rows, full = queries.shape
    group_rows = cluster_of.shape[0]
    width = full // head_count
    half = width // 2
    combos = 4 * half // DH
    owned_count = group_rows // CLUSTER
    mean_slots = group_rows // seq_count
    capacity = mean_slots + mean_slots // 4
    slots = seq_count * capacity
    side = TILE * combos
    mean_rows = owned_count * combos
    mean_count = seq_count * owned_count
    mean_buf_rows = -(-seq_count * mean_rows // side) * side
    line_rows = seq_count // plane * mean_rows
    vmem = pltpu.VMEM
    scratch = [
        vmem((1, group_rows), jnp.int32),
        vmem((1, group_rows), jnp.int32),
        vmem((2, 4, group_rows, half), BF16),
        vmem((4, slots, half), BF16),
        vmem((2, slots * combos, DH), BF16),
        vmem((2, slots * combos, DH), BF16),
        vmem((4, group_rows, half), BF16),
        vmem((4, slots, half), BF16),
        vmem((mean_rows, DH), F32),
        vmem((mean_buf_rows, DH), BF16),
        vmem((combos, mean_buf_rows // combos, DH), BF16),
        vmem((4, slots, half), BF16),
        vmem((4, group_rows, half), BF16),
        vmem((4, group_rows, half), F32),
        vmem((combos, mean_count, DH), F32),
        vmem((seq_count * mean_rows, DH), F32),
        vmem((seq_count * mean_rows, DH), F32),
        vmem((line_rows, DH), F32),
        vmem((line_rows, DH), F32),
        vmem((mean_rows, DH), F32),
        vmem((2, slots * combos, DH), BF16),
        vmem((2, slots * combos, DH), BF16),
        vmem((2, 4, group_rows, half), BF16),
        vmem((slots, group_rows), BF16),
        vmem((group_rows, slots), BF16),
        vmem((slots, group_rows), BF16),
        vmem((group_rows, slots), BF16),
        vmem((slots, group_rows), BF16),
        vmem((group_rows, slots), BF16),
        vmem((side, side), BF16),
        vmem((side, side), BF16),
        vmem((group_rows, slots), F32),
    ]
    dma = pltpu.SemaphoreType.DMA
    by_chunk, by_flow, by_part = dma((2,)), dma((3,)), dma((3, PARTS))
    scratch += [by_chunk] * 3 + [by_flow, by_part] * 2 + [by_chunk] * 3 + [dma] * 8
    scratch += [pltpu.SemaphoreType.REGULAR]
    in_hbm = pl.BlockSpec(memory_space=pltpu.HBM)
    staged = pl.pallas_call(
        functools.partial(kernel, seq_count, head_count, plane, capacity),
        out_shape=jax.ShapeDtypeStruct((4, rows, full), BF16),
        in_specs=[in_hbm] * 6,
        out_specs=in_hbm,
        scratch_shapes=scratch,
        compiler_params=pltpu.CompilerParams(
            collective_id=0, has_side_effects=True, vmem_limit_bytes=63 * 1024 * 1024
        ),
    )(
        queries,
        key_rows,
        value_rows,
        cotangent,
        cluster_of.reshape(1, group_rows),
        order_tokens.reshape(1, group_rows),
    )
    return tuple(staged[i] for i in range(4))


def solution(mesh):
    rows = P(("seq", "head"), None)
    return jax.shard_map(
        per_device,
        mesh=mesh,
        in_specs=(rows,) * 4 + (P("seq"),) * 2,
        out_specs=(rows,) * 4,
        check_vma=False,
    )
```
